512 devices in a mesh: node: 64 (over y, z), cores: 8 (over x, core).
Axes of the slice: x: 4, y: 8, z: 8, core: 2. Of those that a mesh axis runs over, the one named last changes fastest.
Arguments:
- block_state: float32 [1024, 5, 4096], P(('node', 'cores')), as said below
- levels: int32 [1024], P(('node', 'cores')), may hold values from 0 to 3
- send_table: int32 [5, 25088], P(None, ('node', 'cores')), may hold values from 0 to 5, as said below
- receive_table: int32 [24576], P(('node', 'cores')), may hold values from 0 to 48, as said below
- migration: int32 [1024], P(('node', 'cores')), may hold values from 0 to 1023, as said below
- coarsen_flags: int32 [1024], P(('node', 'cores')), may hold values 0 or 1
Outputs:
- new_state: float32 [1024, 5, 4096], P(('node', 'cores'))
The draws below stay inside these ranges and needn't reach their ends.
Inputs may be any that keep to these rules, and one draw needn't show every extreme that they name: `block_state`: densities lie between 0.86 and 1.17, every velocity component is at most 0.9 in magnitude, pressures are positive. `send_table`: Rows: block of the sending device (0 to 1), face (0 to 5), kind (0 same level, 1 sender coarser, 2 sender finer), first and second sub-window (0 to 3; below 2 for kind 0; 0 for kind 2). Entry k of a device is meant for the device k // 7 - 3 further along the curve, cyclically; entries no code names are unused. `receive_table`: the codes of one device are distinct; code c names the device c // 7 - 3 further along the curve, cyclically. On every device some curve offset uses all 7 positions. `migration`: A permutation of the blocks. Each position takes a block of its own device or of an adjacent device (index one lower or higher, no wrap), at most 1 from each neighbour; some device takes exactly 1 from its upper neighbour.
All inputs are finite; a program needn't handle non-finite values. No bound on the sum of `coarsen_flags` on one device may be relied on, other than what follows from the above.
Results may differ from the reference program's by a relative error of at most 0.0003.
Values sent between devices are 32-bit elements; how exact they have to be, the bound alone decides.
A program may use at most 64 MiB of HBM per device.

```python
import jax
import jax.numpy as jnp
import numpy as np
from jax import lax

EDGE = 16
BLOCKS_DEV = 2
LEVELS = 4
REACH = 3
CAP = 7
SEND_SLOTS = 49
HALF = 1
BLOCKS = 1024
N_NODE = 64
N_CORES = 8


def draw_block_state(key, part):
    key = jax.random.fold_in(key, 11)
    subkeys = jax.random.split(key, 3)
    devices = N_NODE * N_CORES
    cells = EDGE * EDGE * EDGE
    owner_index = (jnp.arange(BLOCKS) // BLOCKS_DEV).astype(jnp.float32)
    growth = jnp.exp(jnp.log(9.0) * owner_index / (devices - 1))
    density = jnp.exp(jax.random.uniform(subkeys[0], (BLOCKS, cells), jnp.float32, -0.15, 0.15))
    velocity = jnp.clip(0.4 * jax.random.normal(subkeys[1], (BLOCKS, 3, cells), jnp.float32), -0.9, 0.9)
    pressure = growth[:, None] * jnp.exp(jax.random.uniform(subkeys[2], (BLOCKS, cells), jnp.float32, -0.5, 0.5))
    momentum = density[:, None] * velocity
    energy = pressure / 0.4 + 0.5 * density * jnp.sum(velocity * velocity, 1)
    return jnp.concatenate([density[:, None], momentum, energy[:, None]], 1)


def draw_levels(key, part):
    key = jax.random.fold_in(key, 23)
    drawn = jax.random.randint(key, (BLOCKS,), 0, LEVELS - 1)
    return drawn.at[BLOCKS - BLOCKS_DEV].set(LEVELS - 1).astype(jnp.int32)


def draw_send_table(key, part):
    key = jax.random.fold_in(key, 37)
    subkeys = jax.random.split(key, 5)
    entry_count = N_NODE * N_CORES * SEND_SLOTS
    block_index = jax.random.randint(subkeys[0], (entry_count,), 0, BLOCKS_DEV)
    face_index = jax.random.randint(subkeys[1], (entry_count,), 0, 6)
    kind_index = jax.random.randint(subkeys[2], (entry_count,), 0, 3)
    first_sub = jax.random.randint(subkeys[3], (entry_count,), 0, 4)
    second_sub = jax.random.randint(subkeys[4], (entry_count,), 0, 4)
    first_sub = jnp.where(kind_index == 0, first_sub % 2, jnp.where(kind_index == 2, 0, first_sub))
    second_sub = jnp.where(kind_index == 0, second_sub % 2, jnp.where(kind_index == 2, 0, second_sub))
    return jnp.stack([block_index, face_index, kind_index, first_sub, second_sub], 0).astype(jnp.int32)


def draw_receive_table(key, part):
    key = jax.random.fold_in(key, 41)
    devices = N_NODE * N_CORES
    positions = (2 * REACH + 1) * CAP
    subkeys = jax.random.split(key, devices)
    orders = jax.vmap(lambda single: jax.random.permutation(single, positions))(subkeys)
    return orders[:, :BLOCKS_DEV * 24].reshape(-1).astype(jnp.int32)


def draw_migration(key, part):
    key = jax.random.fold_in(key, 53)
    subkeys = jax.random.split(key, 3)
    devices = N_NODE * N_CORES
    device_range = jnp.arange(devices)
    moved_count = jax.random.randint(subkeys[0], (devices,), 0, HALF + 1)
    forced = jax.random.randint(subkeys[1], (), 0, devices - 1)
    moved_count = jnp.where(device_range == forced, HALF, moved_count)
    moved_count = jnp.where(device_range == devices - 1, 0, moved_count)
    owner_index = device_range[:, None]
    position = jnp.arange(BLOCKS_DEV)[None, :]
    previous = jnp.concatenate([jnp.zeros((1,), moved_count.dtype), moved_count[:-1]])[:, None]
    current = moved_count[:, None]
    source = owner_index * BLOCKS_DEV + position
    source = jnp.where(position >= BLOCKS_DEV - current, (owner_index + 1) * BLOCKS_DEV + position - (BLOCKS_DEV - current), source)
    source = jnp.where(position < previous, (owner_index - 1) * BLOCKS_DEV + BLOCKS_DEV - previous + position, source)
    shuffle = jax.vmap(lambda single: jax.random.permutation(single, BLOCKS_DEV))(jax.random.split(subkeys[2], devices))
    return jnp.take_along_axis(source, shuffle, 1).reshape(-1).astype(jnp.int32)


def plant(values, rng, least, largest):
    longest = values.shape.index(max(values.shape))
    spots = []
    for shift in (0, 1):
        where = [jax.random.randint(jax.random.fold_in(rng, axis), (), 0, length) for axis, length in enumerate(values.shape)]
        where[longest] = (where[longest] + shift) % values.shape[longest]
        spots.append(tuple(where))
    return values.at[spots[0]].set(least).at[spots[1]].set(largest)


def block_scale(own_key, extent, shards, smallest, top_value):
    gain = 1.0
    for dim, blocks in shards:
        heights = jax.random.uniform(jax.random.fold_in(jax.random.fold_in(own_key, 6), dim), (blocks,), jnp.float32, smallest / len(shards), top_value / len(shards))
        gain = gain * jnp.repeat(jnp.exp(heights), extent[dim] // blocks).reshape((-1,) + (1,) * (len(extent) - 1 - dim))
    return gain


def setup_inputs(seed: int = 0) -> dict:
    splits = jax.random.split(jax.random.key(seed), 7)
    return {
        "block_state": draw_block_state(jax.random.fold_in(splits[6], 71), 0),
        "levels": draw_levels(jax.random.fold_in(splits[6], 71), 0),
        "send_table": draw_send_table(jax.random.fold_in(splits[6], 71), 0),
        "receive_table": draw_receive_table(jax.random.fold_in(splits[6], 71), 0),
        "migration": draw_migration(jax.random.fold_in(splits[6], 71), 0),
        "coarsen_flags": plant((jax.random.randint(splits[5], (BLOCKS,), 0, 3) < 1).astype(jnp.int32), jax.random.fold_in(splits[5], 1), 0, 1),
    }


gamma_gas = 1.4
courant = 0.4
weno_eps = 1e-06
highest = lax.Precision.HIGHEST

def predict_table(coarse_count):
    weights = np.zeros((2 * coarse_count, coarse_count))
    for column in range(coarse_count):
        weights[2 * column, column] = 1.0
        odd_row = 2 * column + 1
        if column == 0:
            weights[odd_row, 0:4] = np.array([5.0, 15.0, -5.0, 1.0]) / 16.0
        elif column == coarse_count - 2:
            weights[odd_row, coarse_count - 4:coarse_count] = np.array([1.0, -5.0, 15.0, 5.0]) / 16.0
        elif column == coarse_count - 1:
            weights[odd_row, coarse_count - 1] = 1.0
        else:
            weights[odd_row, column - 1:column + 3] = np.array([-1.0, 9.0, 9.0, -1.0]) / 16.0
    return weights

def slab_tables(edge_cells):
    half_edge = edge_cells // 2
    coarse_rows = predict_table(half_edge)
    fine_rows = predict_table(edge_cells)
    identity = np.eye(edge_cells)
    depth_rows = np.zeros((3, 3, 5))
    depth_rows[0, :, 0:3] = np.eye(3)
    depth_rows[1, :, 0:4] = coarse_rows[0:3, 0:4]
    depth_rows[2, 0, 0] = 1.0
    depth_rows[2, 1, 2] = 1.0
    depth_rows[2, 2, 4] = 1.0
    tangent_rows = np.zeros((3, 4, half_edge, edge_cells))
    for sub_index in range(4):
        lower_row = half_edge * (sub_index % 2)
        tangent_rows[0, sub_index] = identity[lower_row:lower_row + half_edge]
        tangent_rows[1, sub_index] = fine_rows[half_edge * sub_index:half_edge * sub_index + half_edge]
        tangent_rows[2, sub_index] = identity[0::2]
    return (depth_rows, tangent_rows)

def projection_table(edge_cells):
    return predict_table(edge_cells // 2) @ np.eye(edge_cells)[0::2]

def face_layers(blocks, edge_cells):
    lower_x = blocks[:, :, 0:5]
    upper_x = jnp.flip(blocks[:, :, edge_cells - 5:], 2)
    lower_y = jnp.transpose(blocks[:, :, :, 0:5], (0, 1, 3, 2, 4))
    upper_y = jnp.transpose(jnp.flip(blocks[:, :, :, edge_cells - 5:], 3), (0, 1, 3, 2, 4))
    lower_z = jnp.transpose(blocks[:, :, :, :, 0:5], (0, 1, 4, 2, 3))
    upper_z = jnp.transpose(jnp.flip(blocks[:, :, :, :, edge_cells - 5:], 4), (0, 1, 4, 2, 3))
    return jnp.stack([lower_x, upper_x, lower_y, upper_y, lower_z, upper_z], 1)

def make_slabs(blocks, entries, edge_cells):
    half_edge = edge_cells // 2
    depth_np, tangent_np = slab_tables(edge_cells)
    depth_table = jnp.asarray(depth_np.reshape(3, 15), jnp.float32)
    tangent_table = jnp.asarray(tangent_np.reshape(12, half_edge * edge_cells), jnp.float32)
    face_stack = face_layers(blocks, edge_cells).reshape(-1, 5, 5, edge_cells, edge_cells)
    chosen = jnp.take(face_stack, entries[0] * 6 + entries[1], axis=0)
    depth_pick = jnp.dot(jax.nn.one_hot(entries[2], 3, dtype=jnp.float32), depth_table, precision=highest).reshape(-1, 3, 5)
    first_pick = jnp.dot(jax.nn.one_hot(entries[2] * 4 + entries[3], 12, dtype=jnp.float32), tangent_table, precision=highest).reshape(-1, half_edge, edge_cells)
    second_pick = jnp.dot(jax.nn.one_hot(entries[2] * 4 + entries[4], 12, dtype=jnp.float32), tangent_table, precision=highest).reshape(-1, half_edge, edge_cells)
    layered = jnp.einsum('eil,eflab->efiab', depth_pick, chosen, precision=highest)
    layered = jnp.einsum('epa,efiab->efipb', first_pick, layered, precision=highest)
    layered = jnp.einsum('eqb,efipb->efipq', second_pick, layered, precision=highest)
    return layered.reshape(layered.shape[0], -1)

def ghost_faces(ghost_slabs, block_count, edge_cells):
    half_edge = edge_cells // 2
    quarters = ghost_slabs.reshape(block_count, 6, 2, 2, 5, 3, half_edge, half_edge)
    quarters = jnp.transpose(quarters, (0, 1, 4, 5, 2, 6, 3, 7))
    return quarters.reshape(block_count, 6, 5, 3, edge_cells, edge_cells)

def from_cells(blocks, axis_number):
    if axis_number == 1:
        return jnp.transpose(blocks, (0, 1, 3, 2, 4))
    if axis_number == 2:
        return jnp.transpose(blocks, (0, 1, 4, 2, 3))
    return blocks

def to_cells(values, axis_number, edge_cells):
    cube = values.reshape(values.shape[0], 5, edge_cells, edge_cells, edge_cells)
    if axis_number == 1:
        return jnp.transpose(cube, (0, 1, 3, 2, 4))
    if axis_number == 2:
        return jnp.transpose(cube, (0, 1, 3, 4, 2))
    return cube

def extended(blocks, ghosts, axis_number, edge_cells):
    block_count = blocks.shape[0]
    plane = edge_cells * edge_cells
    interior = from_cells(blocks, axis_number).reshape(block_count, 5, edge_cells, plane)
    lower_rim = jnp.flip(ghosts[:, 2 * axis_number], 2).reshape(block_count, 5, 3, plane)
    upper_rim = ghosts[:, 2 * axis_number + 1].reshape(block_count, 5, 3, plane)
    return jnp.concatenate([lower_rim, interior, upper_rim], 2)

def euler_flux(conserved, axis_number):
    density = conserved[:, 0]
    momentum = conserved[:, 1:4]
    energy = conserved[:, 4]
    velocity = momentum / density[:, None]
    pressure = (gamma_gas - 1.0) * (energy - 0.5 * lax.optimization_barrier(jnp.sum(momentum * velocity, 1)))
    normal_velocity = velocity[:, axis_number]
    unit_vector = jnp.asarray(np.eye(3)[axis_number], jnp.float32)[None, :, None, None]
    momentum_flux = momentum * normal_velocity[:, None] + pressure[:, None] * unit_vector
    energy_flux = (energy + pressure) * normal_velocity
    return jnp.concatenate([momentum[:, axis_number][:, None], momentum_flux, energy_flux[:, None]], 1)

def weno_face(far_left, near_left, centre, near_right, far_right):
    candidate_a = (2.0 * far_left - 7.0 * near_left + 11.0 * centre) / 6.0
    candidate_b = (-near_left + 5.0 * centre + 2.0 * near_right) / 6.0
    candidate_c = (2.0 * centre + 5.0 * near_right - far_right) / 6.0
    curve_a = far_left - 2.0 * near_left + centre
    slope_a = far_left - 4.0 * near_left + 3.0 * centre
    curve_b = near_left - 2.0 * centre + near_right
    slope_b = near_left - near_right
    curve_c = centre - 2.0 * near_right + far_right
    slope_c = 3.0 * centre - 4.0 * near_right + far_right
    smooth_a = weno_eps + 13.0 / 12.0 * curve_a * curve_a + 0.25 * slope_a * slope_a
    smooth_b = weno_eps + 13.0 / 12.0 * curve_b * curve_b + 0.25 * slope_b * slope_b
    smooth_c = weno_eps + 13.0 / 12.0 * curve_c * curve_c + 0.25 * slope_c * slope_c
    weight_a = 0.1 / (smooth_a * smooth_a)
    weight_b = 0.6 / (smooth_b * smooth_b)
    weight_c = 0.3 / (smooth_c * smooth_c)
    return (weight_a * candidate_a + weight_b * candidate_b + weight_c * candidate_c) / (weight_a + weight_b + weight_c)

def flux_divergence(stencil_rows, axis_number, fastest):
    edge_cells = stencil_rows.shape[2] - 6
    fluxes = euler_flux(stencil_rows, axis_number)
    plus_part = 0.5 * (fluxes + fastest * stencil_rows)
    minus_part = 0.5 * (fluxes - fastest * stencil_rows)

    def window_at(values, first_cell):
        return values[:, :, first_cell:first_cell + edge_cells + 1]
    numerical = weno_face(window_at(plus_part, 0), window_at(plus_part, 1), window_at(plus_part, 2), window_at(plus_part, 3), window_at(plus_part, 4))
    numerical = numerical + weno_face(window_at(minus_part, 5), window_at(minus_part, 4), window_at(minus_part, 3), window_at(minus_part, 2), window_at(minus_part, 1))
    return numerical[:, :, 1:] - numerical[:, :, :-1]

def inverse_sizes(levels, edge_cells):
    return jnp.left_shift(jnp.ones_like(levels), levels).astype(jnp.float32) * edge_cells

def local_speeds(blocks, levels, edge_cells):
    conserved = blocks.reshape(blocks.shape[0], 5, -1)
    density = conserved[:, 0]
    momentum = conserved[:, 1:4]
    velocity = momentum / density[:, None]
    pressure = (gamma_gas - 1.0) * (conserved[:, 4] - 0.5 * lax.optimization_barrier(jnp.sum(momentum * velocity, 1)))
    sound_speed = jnp.sqrt(gamma_gas * pressure / density)
    wave_speed = lax.optimization_barrier(jnp.max(jnp.abs(velocity), 1)) + sound_speed
    block_fastest = lax.optimization_barrier(jnp.max(wave_speed, 1))
    return (jnp.max(block_fastest), jnp.max(block_fastest * inverse_sizes(levels, edge_cells)))

def advance(blocks, ghost_slabs, levels, fastest, wave_rate, edge_cells):
    ghosts = ghost_faces(ghost_slabs, blocks.shape[0], edge_cells)
    summed = jnp.zeros(blocks.shape, jnp.float32)
    for axis_number in range(3):
        stencil_rows = extended(blocks, ghosts, axis_number, edge_cells)
        summed = summed + to_cells(flux_divergence(stencil_rows, axis_number, fastest), axis_number, edge_cells)
    time_step = courant / wave_rate
    factor = time_step * inverse_sizes(levels, edge_cells)
    return blocks - factor[:, None, None, None, None] * summed

def project_blocks(blocks, edge_cells):
    smoother = jnp.asarray(projection_table(edge_cells), jnp.float32)
    result = jnp.einsum('ia,cfajk->cfijk', smoother, blocks, precision=highest)
    result = jnp.einsum('jb,cfibk->cfijk', smoother, result, precision=highest)
    return jnp.einsum('kd,cfijd->cfijk', smoother, result, precision=highest)

def reference(block_state, levels, send_table, receive_table, migration, coarsen_flags):
    devices = N_NODE * N_CORES
    blocks_all = block_state.reshape(devices, BLOCKS_DEV, 5, EDGE, EDGE, EDGE)
    entries_all = jnp.transpose(send_table.reshape(5, devices, SEND_SLOTS), (1, 0, 2))
    levels_all = levels.reshape(devices, BLOCKS_DEV)

    def device_slabs(carried):
        return make_slabs(carried[0], carried[1], EDGE)
    slab_rows = lax.map(device_slabs, (blocks_all, entries_all))
    slab_rows = slab_rows.reshape(devices * SEND_SLOTS, -1)

    def device_speeds(carried):
        return local_speeds(carried[0], carried[1], EDGE)
    fast_each, rate_each = lax.map(device_speeds, (blocks_all, levels_all))
    fastest = jnp.max(fast_each)
    wave_rate = jnp.max(rate_each)
    slot_codes = receive_table.reshape(devices, BLOCKS_DEV * 24)
    curve_offset = slot_codes // CAP - REACH
    source_device = (jnp.arange(devices, dtype=jnp.int32)[:, None] + curve_offset) % devices
    slot_index = (source_device * SEND_SLOTS + (REACH - curve_offset) * CAP + slot_codes % CAP).astype(jnp.int32)

    def device_update(carried):
        ghost_slabs = jnp.take(slab_rows, carried[2], axis=0)
        return advance(carried[0], ghost_slabs, carried[1], fastest, wave_rate, EDGE)
    updated = lax.map(device_update, (blocks_all, levels_all, slot_index))
    updated = updated.reshape(BLOCKS, 5, EDGE, EDGE, EDGE)
    migrated = jnp.take(updated, migration, axis=0).reshape(devices, BLOCKS_DEV, 5, EDGE, EDGE, EDGE)

    def device_project(carried):
        flagged = (carried[1] == 1)[:, None, None, None, None]
        return jnp.where(flagged, project_blocks(carried[0], EDGE), carried[0])
    result = lax.map(device_project, (migrated, coarsen_flags.reshape(devices, BLOCKS_DEV)))
    return result.reshape(BLOCKS, 5, EDGE * EDGE * EDGE)
```

```python
import functools

import jax
import jax.numpy as jnp
import numpy as np
from jax import lax
from jax.experimental import pallas as pl
from jax.experimental.pallas import tpu as pltpu
from jax.sharding import PartitionSpec as P

MESH = pl.DeviceIdType.MESH
F32 = jnp.float32
BF16 = jnp.bfloat16
EDGE = 16
REACH = 3
CAP = 7
SLOTS = 49
VM = pl.BlockSpec(memory_space=pltpu.VMEM)
SM = pl.BlockSpec(memory_space=pltpu.SMEM)


def predict_table(n):
    w = np.zeros((2 * n, n))
    for c in range(n):
        w[2 * c, c] = 1.0
        if c == 0:
            w[1, 0:4] = np.array([5.0, 15.0, -5.0, 1.0]) / 16.0
        elif c == n - 2:
            w[2 * c + 1, n - 4 : n] = np.array([1.0, -5.0, 15.0, 5.0]) / 16.0
        elif c == n - 1:
            w[2 * c + 1, n - 1] = 1.0
        else:
            w[2 * c + 1, c - 1 : c + 3] = np.array([-1.0, 9.0, 9.0, -1.0]) / 16.0
    return w


def window_tables():
    depth = np.zeros((3, 3, 5))
    depth[0, :, 0:3] = np.eye(3)
    depth[1, :, 0:4] = predict_table(8)[0:3, 0:4]
    depth[2, 0, 0] = depth[2, 1, 2] = depth[2, 2, 4] = 1.0
    eye, fine = np.eye(16), predict_table(16)
    tangent = np.zeros((3, 4, 8, 16))
    for s in range(4):
        tangent[0, s] = eye[8 * (s % 2) : 8 * (s % 2) + 8]
        tangent[1, s] = fine[8 * s : 8 * s + 8]
        tangent[2, s] = eye[0::2]
    return depth, tangent


def constant_tables():
    depth, tangent = window_tables()
    pairs = [(0, s, 0) for s in range(2)]
    pairs += [(1, s, 2 * t) for s in range(4) for t in range(2)]
    pairs += [(2, 0, 0)]
    cols = []
    for kind, sa, sb in pairs:
        tile = np.zeros((16, 16, 8, 2, 8))
        for parity in range(2):
            tile[:, :, :, parity, :] = np.einsum(
                "pa,qb->abpq", tangent[kind, sa], tangent[kind, sb + parity]
            )
        cols.append(tile.reshape(256, 128))
    cols.append(np.zeros((256, 128)))
    tangents = np.concatenate(cols, 1)
    picks = np.zeros((2, 3, 2, 16, 10, 8))
    for kind in range(3):
        for b in range(2):
            for f in range(5):
                for i in range(3):
                    for layer in range(5):
                        picks[0, kind, b, f * 3 + i, b * 5 + f, layer] = depth[kind, i, layer]
                        picks[1, kind, b, f * 3 + i, b * 5 + f, 7 - layer] = depth[kind, i, layer]
    return tangents, picks.reshape(2, 96, 80)


def three_parts(x):
    high = x.astype(BF16)
    rest = x - high.astype(F32)
    middle = rest.astype(BF16)
    low = (rest - middle.astype(F32)).astype(BF16)
    return high, middle, low


def dot(a, b):
    return jnp.dot(a, b, preferred_element_type=F32)


def slab_kernel(x_ref, send_ref, level_ref, tan_ref, pick_ref, slab_ref, speed_ref, left, wide):
    fast = None
    for b in range(2):
        rho = x_ref[0, b * 5]
        inv = 1.0 / rho
        m = [x_ref[0, b * 5 + 1 + i] for i in range(3)]
        v = [mi * inv for mi in m]
        kinetic = m[0] * v[0] + m[1] * v[1] + m[2] * v[2]
        pressure = 0.4 * (x_ref[0, b * 5 + 4] - 0.5 * kinetic)
        speed = jnp.maximum(jnp.maximum(jnp.abs(v[0]), jnp.abs(v[1])), jnp.abs(v[2]))
        speed = speed + jnp.sqrt(1.4 * pressure * inv)
        top = jnp.max(speed)
        rated = top * lax.shift_left(jnp.int32(EDGE), level_ref[b]).astype(F32)
        fast = top if fast is None else jnp.maximum(fast, top)
        rate = rated if b == 0 else jnp.maximum(rate, rated)
    speed_ref[0:8] = jnp.full((8, 128), fast, F32)
    speed_ref[8:16] = jnp.full((8, 128), rate, F32)
    for g in range(6):
        side = g % 2
        planes = x_ref[g // 2, :, 8 * side : 8 * side + 8, :].reshape(80, 256)
        parts = three_parts(planes)
        rows = sum(dot(pick_ref[side], part) for part in parts)
        for n, part in enumerate(three_parts(rows)):
            for kind in range(3):
                left[kind, n, g * 32 : g * 32 + 32] = part[kind * 32 : kind * 32 + 32]
    for tile in range(6):
        kind = 0 if tile == 0 else 1 if tile < 5 else 2
        weights = tan_ref[:, tile * 256 : tile * 256 + 256]
        out = sum(dot(left[kind, n], weights) for n in range(3))
        wide[2 * tile] = out[:, 0:128].reshape(12, 16, 128)
        if tile < 5:
            wide[2 * tile + 1] = out[:, 128:256].reshape(12, 16, 128)
    lane = lax.broadcasted_iota(jnp.int32, (8, 128), 1)
    even = (lane & 8) == 0

    def entry(k, carry):
        blk, g, kind = send_ref[0, k], send_ref[1, k], send_ref[2, k]
        sa, sb = send_ref[3, k], send_ref[4, k]
        pair = jnp.where(kind == 0, sa % 2, jnp.where(kind == 1, 2 + sa * 2 + sb // 2, 10))
        parity = jnp.where(kind == 2, 0, sb % 2)
        low = wide[pair, g * 2 + blk, 0:8]
        high = wide[pair, g * 2 + blk, 8:16]
        first = jnp.where(even, low, pltpu.roll(high, 8, 1))
        second = jnp.where(even, pltpu.roll(low, 120, 1), high)
        slab_ref[k] = jnp.where(jnp.full((8, 128), parity, jnp.int32) == 0, first, second)
        return carry

    lax.fori_loop(0, SLOTS, entry, 0, unroll=7)


def exchange_kernel(
    nz, n_node, n_core,
    slab_ref, speed_ref, x_ref, recv_ref, mig_ref, level_ref,
    ghost_ref, moved_ref, top_ref,
    got, want_out, want_in, stage_g, stage_x, peak, peaks,
    slab_s, slab_r, want_s, want_r, move_s, move_r, peak_s, peak_r, own_s,
):
    node, core = lax.axis_index("node"), lax.axis_index("cores")
    me = node * n_core + core
    total = n_node * n_core
    ny = n_node // nz
    z, y = node % nz, node // nz

    def along(offset):
        other = (me + offset + total) % total
        return (other // n_core, other % n_core)

    groups = [
        [(node, (core + t) % n_core) for t in range(1, n_core)],
        [(y * nz + (z + t) % nz, core) for t in range(1, nz)],
        [(((y + t) % ny) * nz + z, core) for t in range(1, ny)],
    ]
    offsets = [o for o in range(-REACH, REACH + 1) if o != 0]
    partners = [d for group in groups for d in group] + [along(o) for o in offsets]
    barrier = pltpu.get_barrier_semaphore()
    for d in partners:
        pl.semaphore_signal(barrier, inc=1, device_id=d, device_id_type=MESH)
    peak[0] = speed_ref[...]
    wants = []
    for direction in (1, -1):
        want = jnp.int32(0)
        for j in range(2):
            source = mig_ref[j]
            want = want + jnp.where(source // 2 == me + direction, source % 2, 0)
        wants.append(want)
    for n in range(2):
        want_out[n] = jnp.full((8, 128), wants[n], jnp.int32).astype(F32)
    pl.semaphore_wait(barrier, len(partners))

    def send_peaks(phase):
        copies = []
        base = sum(len(g) for g in groups[:phase])
        for t, d in enumerate(groups[phase]):
            copies.append(
                pltpu.make_async_remote_copy(
                    src_ref=peak.at[phase],
                    dst_ref=peaks.at[base + t],
                    send_sem=peak_s.at[base + t],
                    recv_sem=peak_r.at[base + t],
                    device_id=d,
                    device_id_type=MESH,
                )
            )
        for c in copies:
            c.start()
        return copies

    def take_peaks(phase, copies):
        base = sum(len(g) for g in groups[:phase])
        for c in copies:
            c.wait_recv()
        best = peak[phase]
        for t in range(len(copies)):
            best = jnp.maximum(best, peaks[base + t])
        return best

    first = send_peaks(0)
    own = pltpu.make_async_copy(
        slab_ref.at[pl.ds(REACH * CAP, CAP)], got.at[pl.ds(REACH * CAP, CAP)], own_s
    )
    own.start()
    want_copies = []
    for n, direction in enumerate((1, -1)):
        want_copies.append(
            pltpu.make_async_remote_copy(
                src_ref=want_out.at[n],
                dst_ref=want_in.at[n],
                send_sem=want_s.at[n],
                recv_sem=want_r.at[n],
                device_id=along(direction),
                device_id_type=MESH,
            )
        )
    slab_copies = []
    for n, o in enumerate(offsets):
        slab_copies.append(
            pltpu.make_async_remote_copy(
                src_ref=slab_ref.at[pl.ds((o + REACH) * CAP, CAP)],
                dst_ref=got.at[pl.ds((REACH - o) * CAP, CAP)],
                send_sem=slab_s.at[n],
                recv_sem=slab_r.at[n],
                device_id=along(o),
                device_id_type=MESH,
            )
        )
    for c in want_copies + slab_copies:
        c.start()
    peak[1] = take_peaks(0, first)
    second = send_peaks(1)
    own.wait()
    for c in want_copies + slab_copies:
        c.wait_recv()
    lane = lax.broadcasted_iota(jnp.int32, (8, 128), 1)
    row = lax.broadcasted_iota(jnp.int32, (8, 128), 0)
    even = (lane & 8) == 0
    for b in range(2):
        scale = lax.shift_left(jnp.int32(EDGE), level_ref[b]).astype(F32)
        for g in range(6):
            for qa in range(2):
                at = (b * 6 + g) * 4 + 2 * qa
                left = got[recv_ref[at]]
                right = got[recv_ref[at + 1]]
                low = jnp.where(even, left, pltpu.roll(right, 8, 1))
                high = jnp.where(even, pltpu.roll(left, 120, 1), right)
                high = jnp.where(row == 7, scale, high)
                ghost_ref[b, g, qa, 0:8] = low
                ghost_ref[b, g, qa, 8:16] = high
    for n in range(2):
        second_block = want_in[n][0:1, 0:1] > 0.5
        stage_g[n] = jnp.where(second_block, ghost_ref[1], ghost_ref[0])
        for a in range(3):
            stage_x[n, a] = jnp.where(second_block, x_ref[a, 5:10], x_ref[a, 0:5])
    move_copies = []
    for n, direction in enumerate((-1, 1)):
        for m, (src, dst) in enumerate(
            (
                (stage_g.at[n], ghost_ref.at[3 - n]),
                (stage_x.at[n], moved_ref.at[1 - n]),
            )
        ):
            move_copies.append(
                pltpu.make_async_remote_copy(
                    src_ref=src,
                    dst_ref=dst,
                    send_sem=move_s.at[2 * n + m],
                    recv_sem=move_r.at[2 * n + m],
                    device_id=along(direction),
                    device_id_type=MESH,
                )
            )
    for c in move_copies:
        c.start()
    peak[2] = take_peaks(1, second)
    third = send_peaks(2)
    top_ref[...] = take_peaks(2, third)
    for c in move_copies:
        c.wait_recv()
    for c in first + second + third + want_copies + slab_copies + move_copies:
        c.wait_send()


def weno(values, centres, mirrored):
    half = 0.5 * (values[1:] - values[:-1])
    bend = half[1:] - half[:-1]
    rough = 1e-6 + (13.0 / 3.0) * (bend * bend)
    third = bend * (1.0 / 3.0)
    lo, n = centres, 9
    gl, gr = half[lo - 1 : lo - 1 + n], half[lo : lo + n]
    bl, bc, br = (slice(lo - 2 + t, lo - 2 + t + n) for t in range(3))
    tl = 2.0 * gl + bend[bl]
    tc = gl + gr
    tr = 2.0 * gr - bend[br]
    sl = rough[bl] + tl * tl
    sc = rough[bc] + tc * tc
    sr = rough[br] + tr * tr
    il = pl.reciprocal(sl, approx=True)
    ic = pl.reciprocal(sc, approx=True)
    ir = pl.reciprocal(sr, approx=True)
    wl, wc, wr = il * il, 6.0 * (ic * ic), ir * ir
    if mirrored:
        wl = 3.0 * wl
        cl = third[bl] + gl
        cc = third[bc] + gl
        cr = gr - 2.0 * third[br]
        total = wl * cl + wc * cc + wr * cr
        sign = -1.0
    else:
        wr = 3.0 * wr
        cl = gl + 2.0 * third[bl]
        cc = gr - third[bc]
        cr = gr - third[br]
        total = wl * cl + wc * cc + wr * cr
        sign = 1.0
    share = total * pl.reciprocal(wl + wc + wr, approx=True)
    centre = values[lo : lo + n]
    return centre + share if sign > 0 else centre - share


def update_kernel(
    x_ref, moved_ref, ghost_ref, top_ref, slot_ref, out_ref,
    cells, rims, plus, minus, change,
):
    rows = cells
    for b in range(2):
        slot = slot_ref[b]
        own = slot < 2
        for a in range(3):
            for f in range(5):
                base = (a * 5 + f) * 14 * 8
                mine = x_ref[a, jnp.minimum(slot, 1) * 5 + f]
                theirs = moved_ref[jnp.maximum(slot, 2) - 2, a, f]
                v = jnp.where(own, mine, theirs)
                for h in range(2):
                    low = v[0:8, h * 128 : h * 128 + 128]
                    high = v[8:16, h * 128 : h * 128 + 128]
                    r0, r1 = b * 2 + h, 4 + b * 2 + h
                    rows[pl.ds(base + 24 + r0, 8, stride=8), :] = low
                    rows[pl.ds(base + 88 + r0, 3, stride=8), :] = high[0:3]
                    rows[pl.ds(base + r1, 3, stride=8), :] = low[5:8]
                    rows[pl.ds(base + 24 + r1, 8, stride=8), :] = high
        for g in range(6):
            for h in range(2):
                base = (g // 2) * 128 + (g % 2) * 4 + b * 2 + h
                rims[pl.ds(base, 8, stride=8), :] = ghost_ref[slot, g, h, 0:8]
                rims[pl.ds(base + 64, 8, stride=8), :] = ghost_ref[slot, g, h, 8:16]
    for a in range(3):
        for f in range(5):
            base = (a * 5 + f) * 14 * 8
            for layer in range(3):
                rim = rims[pl.ds(a * 128 + (f * 3 + layer) * 8, 8), :]
                rows[pl.ds(base + (2 - layer) * 8, 4), :] = rim[0:4]
                rows[pl.ds(base + (11 + layer) * 8 + 4, 4), :] = rim[4:8]
    fastest = top_ref[0:8]
    step = 0.4 / top_ref[8:16]
    factor = step * rims[pl.ds(15 * 8, 8), :]
    for a in range(3):

        def flux(p, carry):
            u = [rows[pl.ds(pl.multiple_of(((a * 5 + f) * 14 + p) * 8, 8), 8), :] for f in range(5)]
            inv = 1.0 / u[0]
            v = [u[1 + i] * inv for i in range(3)]
            kinetic = u[1] * v[0] + u[2] * v[1] + u[3] * v[2]
            pressure = 0.4 * (u[4] - 0.5 * kinetic)
            flow = [u[1 + a]] + [u[1 + i] * v[a] for i in range(3)] + [(u[4] + pressure) * v[a]]
            flow[1 + a] = flow[1 + a] + pressure
            for f in range(5):
                plus[f, p] = 0.5 * (flow[f] + fastest * u[f])
                minus[f, p] = 0.5 * (flow[f] - fastest * u[f])
            return carry

        lax.fori_loop(0, 14, flux, 0, unroll=2)

        def field(f, carry):
            hat = weno(plus[f], 2, False) + weno(minus[f], 3, True)
            change[a, f] = factor * (hat[1:] - hat[:-1])
            return carry

        lax.fori_loop(0, 5, field, 0)
    for b in range(2):
        for a in range(3):
            for f in range(5):
                for half in range(2):
                    for h in range(2):
                        v = change[a, f, :, half * 4 + b * 2 + h, :]
                        if a == 0:
                            base = f * 14 * 8 + half * 4 + b * 2 + h
                            u = rows[pl.ds(base + 24, 8, stride=8), :]
                            v = u - v
                        out_ref[a, b * 5 + f, half * 8 : half * 8 + 8, h * 128 : h * 128 + 128] = v


def solution(mesh):
    n_node, n_core = mesh.shape["node"], mesh.shape["cores"]
    nz = max(1, int(round(n_node**0.5)))
    tangents, picks = constant_tables()
    smoother = predict_table(8) @ np.eye(16)[0::2]
    plane_smoother = np.kron(smoother, smoother)
    highest = lax.Precision.HIGHEST
    groups = n_core - 1 + nz - 1 + n_node // nz - 1

    def body(block_state, levels, send_table, receive_table, migration, coarsen_flags):
        cube = block_state.reshape(10, 16, 16, 16)
        x = jnp.stack(
            [
                cube.reshape(10, 16, 256),
                jnp.transpose(cube, (0, 2, 1, 3)).reshape(10, 16, 256),
                jnp.transpose(cube, (0, 3, 1, 2)).reshape(10, 16, 256),
            ]
        )
        slabs, speeds = pl.pallas_call(
            slab_kernel,
            out_shape=(
                jax.ShapeDtypeStruct((SLOTS, 8, 128), F32),
                jax.ShapeDtypeStruct((16, 128), F32),
            ),
            in_specs=[VM, SM, SM, VM, VM],
            out_specs=(VM, VM),
            scratch_shapes=[
                pltpu.VMEM((3, 3, 192, 256), BF16),
                pltpu.VMEM((11, 12, 16, 128), F32),
            ],
            compiler_params=pltpu.CompilerParams(vmem_limit_bytes=48 << 20),
            name="slabs",
        )(x, send_table, levels, jnp.asarray(tangents, BF16), jnp.asarray(picks, BF16))
        ghosts, moved, top = pl.pallas_call(
            functools.partial(exchange_kernel, nz, n_node, n_core),
            out_shape=(
                jax.ShapeDtypeStruct((4, 6, 2, 16, 128), F32),
                jax.ShapeDtypeStruct((2, 3, 5, 16, 256), F32),
                jax.ShapeDtypeStruct((16, 128), F32),
            ),
            in_specs=[VM, VM, VM, SM, SM, SM],
            out_specs=(VM, VM, VM),
            scratch_shapes=[
                pltpu.VMEM((SLOTS, 8, 128), F32),
                pltpu.VMEM((2, 8, 128), F32),
                pltpu.VMEM((2, 8, 128), F32),
                pltpu.VMEM((2, 6, 2, 16, 128), F32),
                pltpu.VMEM((2, 3, 5, 16, 256), F32),
                pltpu.VMEM((3, 16, 128), F32),
                pltpu.VMEM((groups, 16, 128), F32),
                pltpu.SemaphoreType.DMA((6,)),
                pltpu.SemaphoreType.DMA((6,)),
                pltpu.SemaphoreType.DMA((2,)),
                pltpu.SemaphoreType.DMA((2,)),
                pltpu.SemaphoreType.DMA((4,)),
                pltpu.SemaphoreType.DMA((4,)),
                pltpu.SemaphoreType.DMA((groups,)),
                pltpu.SemaphoreType.DMA((groups,)),
                pltpu.SemaphoreType.DMA,
            ],
            compiler_params=pltpu.CompilerParams(
                collective_id=0, has_side_effects=True, vmem_limit_bytes=48 << 20
            ),
            name="exchange",
        )(slabs, speeds, x, receive_table, migration, levels)
        me = lax.axis_index("node") * n_core + lax.axis_index("cores")
        source = migration // 2
        slot = jnp.where(source == me, migration % 2, jnp.where(source < me, 2, 3)).astype(jnp.int32)
        parts = pl.pallas_call(
            update_kernel,
            out_shape=jax.ShapeDtypeStruct((3, 10, 16, 256), F32),
            in_specs=[VM, VM, VM, VM, SM],
            out_specs=VM,
            scratch_shapes=[
                pltpu.VMEM((3 * 5 * 14 * 8, 128), F32),
                pltpu.VMEM((3 * 16 * 8, 128), F32),
                pltpu.VMEM((5, 14, 8, 128), F32),
                pltpu.VMEM((5, 14, 8, 128), F32),
                pltpu.VMEM((3, 5, 8, 8, 128), F32),
            ],
            compiler_params=pltpu.CompilerParams(vmem_limit_bytes=48 << 20),
            name="update",
        )(x, moved, ghosts, top, slot)
        second = jnp.transpose(parts[1].reshape(10, 16, 16, 16), (0, 2, 1, 3)).reshape(10, 16, 256)
        third = jnp.transpose(parts[2].reshape(10, 16, 16, 16), (0, 2, 3, 1)).reshape(10, 16, 256)
        migrated = parts[0] - second - third
        smooth = jnp.einsum(
            "nim,mt->nit", migrated, jnp.asarray(plane_smoother.T, F32), precision=highest
        )
        smooth = jnp.einsum("ia,nam->nim", jnp.asarray(smoother, F32), smooth, precision=highest)
        flagged = jnp.repeat(coarsen_flags == 1, 5)[:, None, None]
        result = jnp.where(flagged, smooth, migrated)
        return result.reshape(2, 5, 4096)

    both = ("node", "cores")
    return jax.shard_map(
        body,
        mesh=mesh,
        in_specs=(P(both, None, None), P(both), P(None, both), P(both), P(both), P(both)),
        out_specs=P(both, None, None),
        check_vma=False,
    )
```

```python
import functools

import jax
import jax.numpy as jnp
import numpy as np
from jax import lax
from jax.experimental import pallas as pl
from jax.experimental.pallas import tpu as pltpu
from jax.sharding import PartitionSpec as P

MESH = pl.DeviceIdType.MESH
F32 = jnp.float32
BF16 = jnp.bfloat16
EDGE = 16
REACH = 3
CAP = 7
SLOTS = 49
VM = pl.BlockSpec(memory_space=pltpu.VMEM)
SM = pl.BlockSpec(memory_space=pltpu.SMEM)
HB = pl.BlockSpec(memory_space=pltpu.HBM)


def predict_table(n):
    w = np.zeros((2 * n, n))
    for c in range(n):
        w[2 * c, c] = 1.0
        if c == 0:
            w[1, 0:4] = np.array([5.0, 15.0, -5.0, 1.0]) / 16.0
        elif c == n - 2:
            w[2 * c + 1, n - 4 : n] = np.array([1.0, -5.0, 15.0, 5.0]) / 16.0
        elif c == n - 1:
            w[2 * c + 1, n - 1] = 1.0
        else:
            w[2 * c + 1, c - 1 : c + 3] = np.array([-1.0, 9.0, 9.0, -1.0]) / 16.0
    return w


def window_tables():
    depth = np.zeros((3, 3, 5))
    depth[0, :, 0:3] = np.eye(3)
    depth[1, :, 0:4] = predict_table(8)[0:3, 0:4]
    depth[2, 0, 0] = depth[2, 1, 2] = depth[2, 2, 4] = 1.0
    eye, fine = np.eye(16), predict_table(16)
    tangent = np.zeros((3, 4, 8, 16))
    for s in range(4):
        tangent[0, s] = eye[8 * (s % 2) : 8 * (s % 2) + 8]
        tangent[1, s] = fine[8 * s : 8 * s + 8]
        tangent[2, s] = eye[0::2]
    return depth, tangent


def constant_tables():
    depth, tangent = window_tables()
    pairs = [(0, s, 0) for s in range(2)]
    pairs += [(1, s, 2 * t) for s in range(4) for t in range(2)]
    pairs += [(2, 0, 0)]
    cols = []
    for kind, sa, sb in pairs:
        tile = np.zeros((16, 16, 8, 2, 8))
        for parity in range(2):
            tile[:, :, :, parity, :] = np.einsum(
                "pa,qb->abpq", tangent[kind, sa], tangent[kind, sb + parity]
            )
        cols.append(tile.reshape(256, 128))
    cols.append(np.zeros((256, 128)))
    tangents = np.concatenate(cols, 1)
    picks = np.zeros((2, 3, 2, 16, 10, 8))
    for kind in range(3):
        for b in range(2):
            for f in range(5):
                for i in range(3):
                    for layer in range(5):
                        picks[0, kind, b, f * 3 + i, b * 5 + f, layer] = depth[kind, i, layer]
                        picks[1, kind, b, f * 3 + i, b * 5 + f, 7 - layer] = depth[kind, i, layer]
    return tangents, picks.reshape(2, 96, 80)


def three_parts(x):
    high = x.astype(BF16)
    rest = x - high.astype(F32)
    middle = rest.astype(BF16)
    low = (rest - middle.astype(F32)).astype(BF16)
    return high, middle, low


def dot(a, b):
    return jnp.dot(a, b, preferred_element_type=F32)


def iotas():
    lane = lax.broadcasted_iota(jnp.int32, (8, 128), 1)
    row = lax.broadcasted_iota(jnp.int32, (8, 128), 0)
    return lane, row


def swap(planes, lane, bit, reach):
    keep = (lane & reach) == 0
    out = list(planes)
    for v in range(8):
        if not (v >> bit) & 1:
            w = v | (1 << bit)
            out[v] = jnp.where(keep, planes[v], pltpu.roll(planes[w], reach, 1))
            out[w] = jnp.where(keep, pltpu.roll(planes[v], 128 - reach, 1), planes[w])
    return out


def swaps(planes, lane, reach):
    for bit in (2, 1, 0):
        planes = swap(planes, lane, bit, reach << bit)
    return planes


def cross(x, lane, row):
    odd = row & 1
    low = jnp.where(odd == 0, x, pltpu.roll(x, 1, 0))
    high = jnp.where(odd == 0, pltpu.roll(x, 7, 0), x)
    index = (lane & 7) * 16 + odd * 8 + lax.shift_right_logical(lane, 4)
    return jnp.where(
        (lane & 8) == 0,
        jnp.take_along_axis(low, index, axis=1),
        jnp.take_along_axis(high, index, axis=1),
    )


def turned(planes, dim, lane, row):
    if dim == 1:
        return swaps(planes, lane, 16)
    return [cross(x, lane, row) for x in swaps(planes, lane, 1)]


def turned_back(planes, dim, lane, row):
    if dim == 1:
        return swaps(planes, lane, 16)
    return swaps([cross(x, lane, row) for x in planes], lane, 1)


def row_of(dim, half, block, h):
    return half * 4 + block * 2 + h if dim == 0 else h * 4 + block * 2 + half


def plane_rows(ref, dim, half, base=0):
    return jnp.concatenate(
        [
            jnp.concatenate(
                [ref[pl.ds(base + f * 64 + row_of(dim, half, b, h), 8, stride=8), :] for h in range(2)], 1
            )
            for b in range(2)
            for f in range(5)
        ],
        0,
    )


def exchange_kernel(
    nz, n_node, n_core,
    x_ref, send_ref, recv_ref, mig_ref, level_ref, tan_hbm, pick_hbm,
    dense_ref, ghost_ref, moved_ref, top_ref,
    turns, left, wide, slabs, got, want_out, want_in, stage_g, stage_x, peak, peaks,
    tan_ref, pick_ref, slab_s, slab_r, want_s, want_r, move_s, move_r, peak_s, peak_r, load_s,
):
    node, core = lax.axis_index("node"), lax.axis_index("cores")
    me = node * n_core + core
    total = n_node * n_core
    ny = n_node // nz
    z, y = node % nz, node // nz
    lane, row = iotas()

    def along(offset):
        other = (me + offset + total) % total
        return (other // n_core, other % n_core)

    groups = [
        [(node, (core + t) % n_core) for t in range(1, n_core)],
        [(y * nz + (z + t) % nz, core) for t in range(1, nz)],
        [(((y + t) % ny) * nz + z, core) for t in range(1, ny)],
    ]
    offsets = [o for o in range(-REACH, REACH + 1) if o != 0]
    partners = [d for group in groups for d in group] + [along(o) for o in offsets]
    barrier = pltpu.get_barrier_semaphore()
    for d in partners:
        pl.semaphore_signal(barrier, inc=1, device_id=d, device_id_type=MESH)
    load_pick = pltpu.make_async_copy(pick_hbm, pick_ref, load_s.at[0])
    load_tan = pltpu.make_async_copy(tan_hbm, tan_ref, load_s.at[1])
    load_pick.start()
    load_tan.start()

    def send_peaks(phase):
        base = sum(len(g) for g in groups[:phase])
        copies = [
            pltpu.make_async_remote_copy(
                src_ref=peak.at[phase],
                dst_ref=peaks.at[base + t],
                send_sem=peak_s.at[base + t],
                recv_sem=peak_r.at[base + t],
                device_id=d,
                device_id_type=MESH,
            )
            for t, d in enumerate(groups[phase])
        ]
        for c in copies:
            c.start()
        return copies

    def take_peaks(phase, copies):
        base = sum(len(g) for g in groups[:phase])
        for c in copies:
            c.wait_recv()
        best = peak[phase]
        for t in range(len(copies)):
            best = jnp.maximum(best, peaks[base + t])
        return best

    for f in range(5):
        for c in range(32):
            at = f * 64 + (c // 2 % 8) * 8 + (c // 16) * 4 + c % 2
            turns[pl.ds(at, 2, stride=2), :] = x_ref[f, :, c * 128 : c * 128 + 128]
    top = None
    for v in range(8):
        u = [turns[f * 64 + v * 8 : f * 64 + v * 8 + 8] for f in range(5)]
        inv = 1.0 / u[0]
        vel = [u[1 + i] * inv for i in range(3)]
        kinetic = u[1] * vel[0] + u[2] * vel[1] + u[3] * vel[2]
        pressure = 0.4 * (u[4] - 0.5 * kinetic)
        speed = jnp.maximum(jnp.maximum(jnp.abs(vel[0]), jnp.abs(vel[1])), jnp.abs(vel[2]))
        speed = speed + jnp.sqrt(1.4 * pressure * inv)
        top = speed if v == 0 else jnp.maximum(top, speed)
    scales = [lax.shift_left(jnp.int32(EDGE), level_ref[b]).astype(F32) for b in range(2)]
    rated = top * jnp.where((row & 2) == 0, scales[0], scales[1])
    peak[0, 0:8] = jnp.full((8, 128), jnp.max(top), F32)
    peak[0, 8:16] = jnp.full((8, 128), jnp.max(rated), F32)
    for n, direction in enumerate((1, -1)):
        want = jnp.int32(0)
        for j in range(2):
            source = mig_ref[j]
            want = want + jnp.where(source // 2 == me + direction, source % 2, 0)
        want_out[n] = jnp.full((8, 128), want, jnp.int32).astype(F32)
    pl.semaphore_wait(barrier, len(partners))
    first = send_peaks(0)
    want_copies = [
        pltpu.make_async_remote_copy(
            src_ref=want_out.at[n],
            dst_ref=want_in.at[n],
            send_sem=want_s.at[n],
            recv_sem=want_r.at[n],
            device_id=along(direction),
            device_id_type=MESH,
        )
        for n, direction in enumerate((1, -1))
    ]
    for c in want_copies:
        c.start()
    for f in range(5):
        planes = [turns[f * 64 + v * 8 : f * 64 + v * 8 + 8] for v in range(8)]
        for v in range(8):
            dense_ref[f * 64 + v * 8 : f * 64 + v * 8 + 8] = planes[v]
        for dim in (1, 2):
            for v, value in enumerate(turned(planes, dim, lane, row)):
                at = dim * 320 + f * 64 + v * 8
                turns[at : at + 8] = value
    load_pick.wait()
    for g in range(6):
        side = g % 2
        parts = three_parts(plane_rows(turns, g // 2, side, (g // 2) * 320))
        rows = sum(dot(pick_ref[side], part) for part in parts)
        for n, part in enumerate(three_parts(rows)):
            for kind in range(3):
                left[kind, n, g * 32 : g * 32 + 32] = part[kind * 32 : kind * 32 + 32]
    peak[1] = take_peaks(0, first)
    second = send_peaks(1)
    load_tan.wait()
    for tile in range(6):
        kind = 0 if tile == 0 else 1 if tile < 5 else 2
        weights = tan_ref[:, tile * 256 : tile * 256 + 256]
        out = sum(dot(left[kind, n], weights) for n in range(3))
        wide[2 * tile] = out[:, 0:128].reshape(12, 16, 128)
        if tile < 5:
            wide[2 * tile + 1] = out[:, 128:256].reshape(12, 16, 128)
    even = (lane & 8) == 0

    def entry(k, into, at):
        blk, g, kind = send_ref[0, k], send_ref[1, k], send_ref[2, k]
        sa, sb = send_ref[3, k], send_ref[4, k]
        pair = jnp.where(kind == 0, sa % 2, jnp.where(kind == 1, 2 + sa * 2 + sb // 2, 10))
        parity = jnp.where(kind == 2, 0, sb % 2)
        low = wide[pair, g * 2 + blk, 0:8]
        high = wide[pair, g * 2 + blk, 8:16]
        ahead = jnp.where(even, low, pltpu.roll(high, 8, 1))
        behind = jnp.where(even, pltpu.roll(low, 120, 1), high)
        into[at] = jnp.where(jnp.full((8, 128), parity, jnp.int32) == 0, ahead, behind)

    slab_copies = []
    for n, o in enumerate(offsets):
        for m in range(CAP):
            entry((o + REACH) * CAP + m, slabs, n * CAP + m)
        copy = pltpu.make_async_remote_copy(
            src_ref=slabs.at[pl.ds(n * CAP, CAP)],
            dst_ref=got.at[pl.ds((REACH - o) * CAP, CAP)],
            send_sem=slab_s.at[n],
            recv_sem=slab_r.at[n],
            device_id=along(o),
            device_id_type=MESH,
        )
        copy.start()
        slab_copies.append(copy)
    for m in range(CAP):
        entry(REACH * CAP + m, got, REACH * CAP + m)
    peak[2] = take_peaks(1, second)
    third = send_peaks(2)
    for c in want_copies + slab_copies:
        c.wait_recv()
    second_block = [want_in[n] > 0.5 for n in range(2)]
    for n in range(2):
        pick = second_block[n]
        for f in range(5):
            for t in range(4):
                at = f * 64 + t * 16
                one, two = turns[at : at + 8], turns[at + 8 : at + 16]
                one = jnp.where(pick, pltpu.roll(one, 6, 0), one)
                two = jnp.where(pick, two, pltpu.roll(two, 2, 0))
                stage_x[n, f, t] = jnp.where((row & 2) == 0, one, two)
    move_copies = []
    for n, direction in enumerate((-1, 1)):
        for m, (src, dst) in enumerate(
            (
                (stage_x.at[n], moved_ref.at[1 - n]),
                (stage_g.at[n], ghost_ref.at[3 - n]),
            )
        ):
            move_copies.append(
                pltpu.make_async_remote_copy(
                    src_ref=src,
                    dst_ref=dst,
                    send_sem=move_s.at[2 * n + m],
                    recv_sem=move_r.at[2 * n + m],
                    device_id=along(direction),
                    device_id_type=MESH,
                )
            )
    move_copies[0].start()
    move_copies[2].start()
    for g in range(6):
        for qa in range(2):
            pair = []
            for b in range(2):
                at = (b * 6 + g) * 4 + 2 * qa
                one, two = got[recv_ref[at]], got[recv_ref[at + 1]]
                low = jnp.where(even, one, pltpu.roll(two, 8, 1))
                high = jnp.where(even, pltpu.roll(one, 120, 1), two)
                high = jnp.where(row == 7, scales[b], high)
                ghost_ref[b, g, qa, 0:8] = low
                ghost_ref[b, g, qa, 8:16] = high
                pair.append((low, high))
            for n in range(2):
                pick = second_block[n]
                stage_g[n, g, qa, 0:8] = jnp.where(pick, pair[1][0], pair[0][0])
                stage_g[n, g, qa, 8:16] = jnp.where(pick, pair[1][1], pair[0][1])
    move_copies[1].start()
    move_copies[3].start()
    top_ref[...] = take_peaks(2, third)
    for c in move_copies:
        c.wait_recv()
    for c in first + second + third + want_copies + slab_copies + move_copies:
        c.wait_send()


def weno(values, centres, mirrored):
    half = 0.5 * (values[1:] - values[:-1])
    bend = half[1:] - half[:-1]
    rough = 1e-6 + (13.0 / 3.0) * (bend * bend)
    third = bend * (1.0 / 3.0)
    lo, n = centres, 9
    gl, gr = half[lo - 1 : lo - 1 + n], half[lo : lo + n]
    bl, bc, br = (slice(lo - 2 + t, lo - 2 + t + n) for t in range(3))
    tl = 2.0 * gl + bend[bl]
    tc = gl + gr
    tr = 2.0 * gr - bend[br]
    sl = rough[bl] + tl * tl
    sc = rough[bc] + tc * tc
    sr = rough[br] + tr * tr
    il = pl.reciprocal(sl, approx=True)
    ic = pl.reciprocal(sc, approx=True)
    ir = pl.reciprocal(sr, approx=True)
    wl, wc, wr = il * il, 6.0 * (ic * ic), ir * ir
    if mirrored:
        wl = 3.0 * wl
        cl = third[bl] + gl
        cc = third[bc] + gl
        cr = gr - 2.0 * third[br]
        total = wl * cl + wc * cc + wr * cr
        sign = -1.0
    else:
        wr = 3.0 * wr
        cl = gl + 2.0 * third[bl]
        cc = gr - third[bc]
        cr = gr - third[br]
        total = wl * cl + wc * cc + wr * cr
        sign = 1.0
    share = total * pl.reciprocal(wl + wc + wr, approx=True)
    centre = values[lo : lo + n]
    return centre + share if sign > 0 else centre - share


def update_kernel(
    n_core, dense_ref, moved_ref, ghost_ref, top_ref, mig_ref, flag_ref, lane_hbm, line_hbm, out_ref,
    cells, rims, plus, minus, change, result, lane_ref, line_ref, load_s,
):
    load_lane = pltpu.make_async_copy(lane_hbm, lane_ref, load_s.at[0])
    load_line = pltpu.make_async_copy(line_hbm, line_ref, load_s.at[1])
    load_lane.start()
    load_line.start()
    me = lax.axis_index("node") * n_core + lax.axis_index("cores")
    lane, row = iotas()
    slots = []
    for j in range(2):
        source = mig_ref[j]
        far = jnp.where(source // 2 < me, 2, 3)
        slots.append(jnp.where(source // 2 == me, source % 2, far))
    for b in range(2):
        for g in range(6):
            for h in range(2):
                base = (g // 2) * 128 + row_of(g // 2, g % 2, b, h)
                rims[pl.ds(base, 8, stride=8), :] = ghost_ref[slots[b], g, h, 0:8]
                rims[pl.ds(base + 64, 8, stride=8), :] = ghost_ref[slots[b], g, h, 8:16]
    for f in range(5):
        planes = []
        for v in range(8):
            own = dense_ref[f * 64 + v * 8 : f * 64 + v * 8 + 8]
            down, up = moved_ref[0, f, v // 2], moved_ref[1, f, v // 2]
            for b in range(2):
                away = 6 if b == 0 else 2
                mine = jnp.where(slots[b] == b, own, pltpu.roll(own, away, 0))
                other = jnp.where(slots[b] == 2, down, up)
                if v % 2 != b:
                    other = pltpu.roll(other, away, 0)
                value = jnp.where(slots[b] < 2, mine, other)
                both = value if b == 0 else jnp.where((row & 2) == 0, both, value)
            planes.append(both)
        for a in range(3):
            layout = planes if a == 0 else turned(planes, a, lane, row)
            lower = (row & (4 if a == 0 else 1)) == 0
            up, down = (4, 4) if a == 0 else (1, 7)
            for v in range(8):
                cells[a, f, 3 + v] = layout[v]
            for layer in range(3):
                rim = rims[a * 128 + (f * 3 + layer) * 8 : a * 128 + (f * 3 + layer) * 8 + 8]
                cells[a, f, 2 - layer] = jnp.where(lower, rim, pltpu.roll(layout[7 - layer], up, 0))
                cells[a, f, 11 + layer] = jnp.where(lower, pltpu.roll(layout[layer], down, 0), rim)
    fastest = top_ref[0:8]
    step = 0.4 / top_ref[8:16]
    factor = step * rims[120:128]
    for a in range(3):

        def flux(p, carry):
            u = [cells[a, f, p] for f in range(5)]
            inv = 1.0 / u[0]
            v = [u[1 + i] * inv for i in range(3)]
            kinetic = u[1] * v[0] + u[2] * v[1] + u[3] * v[2]
            pressure = 0.4 * (u[4] - 0.5 * kinetic)
            flow = [u[1 + a]] + [u[1 + i] * v[a] for i in range(3)] + [(u[4] + pressure) * v[a]]
            flow[1 + a] = flow[1 + a] + pressure
            for f in range(5):
                plus[f, p] = 0.5 * (flow[f] + fastest * u[f])
                minus[f, p] = 0.5 * (flow[f] - fastest * u[f])
            return carry

        lax.fori_loop(0, 14, flux, 0, unroll=2)

        def field(f, carry):
            hat = weno(plus[f], 2, False) + weno(minus[f], 3, True)
            change[a, f] = hat[1:] - hat[:-1]
            return carry

        lax.fori_loop(0, 5, field, 0)
    for f in range(5):
        second = turned_back([change[1, f, v] for v in range(8)], 1, lane, row)
        third = turned_back([change[2, f, v] for v in range(8)], 2, lane, row)
        for v in range(8):
            moved = change[0, f, v] + second[v] + third[v]
            result[f * 64 + v * 8 : f * 64 + v * 8 + 8] = cells[0, f, 3 + v] - factor * moved

    load_lane.wait()
    load_line.wait()

    @pl.when(jnp.logical_or(flag_ref[0] == 1, flag_ref[1] == 1))
    def _():
        halves = [plane_rows(result, 0, half) for half in range(2)]
        cubes = jnp.concatenate(
            [halves[half][n * 8 : n * 8 + 8] for n in range(10) for half in range(2)], 0
        )
        smooth = sum(dot(part, lane_ref[...]) for part in three_parts(cubes))
        smooth = sum(dot(line_ref[...], part) for part in three_parts(smooth))
        for b in range(2):

            @pl.when(flag_ref[b] == 1)
            def _():
                for f in range(5):
                    for half in range(2):
                        at = (b * 5 + f) * 16 + half * 8
                        for h in range(2):
                            base = f * 64 + row_of(0, half, b, h)
                            result[pl.ds(base, 8, stride=8), :] = smooth[at : at + 8, h * 128 : h * 128 + 128]

    for f in range(5):
        for c in range(32):
            at = f * 64 + (c // 2 % 8) * 8 + (c // 16) * 4 + c % 2
            out_ref[f, :, c * 128 : c * 128 + 128] = result[pl.ds(at, 2, stride=2), :]


def solution(mesh):
    n_node, n_core = mesh.shape["node"], mesh.shape["cores"]
    nz = max(1, int(round(n_node**0.5)))
    tangents, picks = constant_tables()
    smoother = predict_table(8) @ np.eye(16)[0::2]
    lane_smoother = np.kron(smoother, smoother).T
    line_smoother = np.kron(np.eye(10), smoother)
    groups = n_core - 1 + nz - 1 + n_node // nz - 1

    def body(block_state, levels, send_table, receive_table, migration, coarsen_flags):
        dense, ghosts, moved, top = pl.pallas_call(
            functools.partial(exchange_kernel, nz, n_node, n_core),
            out_shape=(
                jax.ShapeDtypeStruct((320, 128), F32),
                jax.ShapeDtypeStruct((4, 6, 2, 16, 128), F32),
                jax.ShapeDtypeStruct((2, 5, 4, 8, 128), F32),
                jax.ShapeDtypeStruct((16, 128), F32),
            ),
            in_specs=[VM, SM, SM, SM, SM, HB, HB],
            out_specs=(VM, VM, VM, VM),
            scratch_shapes=[
                pltpu.VMEM((960, 128), F32),
                pltpu.VMEM((3, 3, 192, 256), BF16),
                pltpu.VMEM((11, 12, 16, 128), F32),
                pltpu.VMEM((SLOTS - CAP, 8, 128), F32),
                pltpu.VMEM((SLOTS, 8, 128), F32),
                pltpu.VMEM((2, 8, 128), F32),
                pltpu.VMEM((2, 8, 128), F32),
                pltpu.VMEM((2, 6, 2, 16, 128), F32),
                pltpu.VMEM((2, 5, 4, 8, 128), F32),
                pltpu.VMEM((3, 16, 128), F32),
                pltpu.VMEM((groups, 16, 128), F32),
                pltpu.VMEM((256, 1536), BF16),
                pltpu.VMEM((2, 96, 80), BF16),
                pltpu.SemaphoreType.DMA((6,)),
                pltpu.SemaphoreType.DMA((6,)),
                pltpu.SemaphoreType.DMA((2,)),
                pltpu.SemaphoreType.DMA((2,)),
                pltpu.SemaphoreType.DMA((4,)),
                pltpu.SemaphoreType.DMA((4,)),
                pltpu.SemaphoreType.DMA((groups,)),
                pltpu.SemaphoreType.DMA((groups,)),
                pltpu.SemaphoreType.DMA((2,)),
            ],
            compiler_params=pltpu.CompilerParams(
                collective_id=0, has_side_effects=True, vmem_limit_bytes=48 << 20
            ),
            name="exchange",
        )(
            jnp.transpose(block_state, (1, 0, 2)), send_table, receive_table, migration, levels,
            jnp.asarray(tangents, BF16), jnp.asarray(picks, BF16),
        )
        state = pl.pallas_call(
            functools.partial(update_kernel, n_core),
            out_shape=jax.ShapeDtypeStruct((5, 2, 4096), F32),
            in_specs=[VM, VM, VM, VM, SM, SM, HB, HB],
            out_specs=VM,
            scratch_shapes=[
                pltpu.VMEM((3, 5, 14, 8, 128), F32),
                pltpu.VMEM((3 * 16 * 8, 128), F32),
                pltpu.VMEM((5, 14, 8, 128), F32),
                pltpu.VMEM((5, 14, 8, 128), F32),
                pltpu.VMEM((3, 5, 8, 8, 128), F32),
                pltpu.VMEM((320, 128), F32),
                pltpu.VMEM((256, 256), BF16),
                pltpu.VMEM((160, 160), BF16),
                pltpu.SemaphoreType.DMA((2,)),
            ],
            compiler_params=pltpu.CompilerParams(vmem_limit_bytes=48 << 20),
            name="update",
        )(
            dense, moved, ghosts, top, migration, coarsen_flags,
            jnp.asarray(lane_smoother, BF16), jnp.asarray(line_smoother, BF16),
        )
        return jnp.transpose(state, (1, 0, 2))

    both = ("node", "cores")
    return jax.shard_map(
        body,
        mesh=mesh,
        in_specs=(P(both, None, None), P(both), P(None, both), P(both), P(both), P(both)),
        out_specs=P(both, None, None),
        check_vma=False,
    )
```

```python
import functools

import jax
import jax.numpy as jnp
import numpy as np
from jax import lax
from jax.experimental import pallas as pl
from jax.experimental.pallas import tpu as pltpu
from jax.sharding import PartitionSpec as P

MESH = pl.DeviceIdType.MESH
F32 = jnp.float32
BF16 = jnp.bfloat16
EDGE = 16
REACH = 3
CAP = 7
VMEM_BYTES = 63 << 20
SLOTS = 49
VM = pl.BlockSpec(memory_space=pltpu.VMEM)
SM = pl.BlockSpec(memory_space=pltpu.SMEM)
HB = pl.BlockSpec(memory_space=pltpu.HBM)


def predict_table(n):
    w = np.zeros((2 * n, n))
    for c in range(n):
        w[2 * c, c] = 1.0
        if c == 0:
            w[1, 0:4] = np.array([5.0, 15.0, -5.0, 1.0]) / 16.0
        elif c == n - 2:
            w[2 * c + 1, n - 4 : n] = np.array([1.0, -5.0, 15.0, 5.0]) / 16.0
        elif c == n - 1:
            w[2 * c + 1, n - 1] = 1.0
        else:
            w[2 * c + 1, c - 1 : c + 3] = np.array([-1.0, 9.0, 9.0, -1.0]) / 16.0
    return w


def window_tables():
    depth = np.zeros((3, 3, 5))
    depth[0, :, 0:3] = np.eye(3)
    depth[1, :, 0:4] = predict_table(8)[0:3, 0:4]
    depth[2, 0, 0] = depth[2, 1, 2] = depth[2, 2, 4] = 1.0
    eye, fine = np.eye(16), predict_table(16)
    tangent = np.zeros((3, 4, 8, 16))
    for s in range(4):
        tangent[0, s] = eye[8 * (s % 2) : 8 * (s % 2) + 8]
        tangent[1, s] = fine[8 * s : 8 * s + 8]
        tangent[2, s] = eye[0::2]
    return depth, tangent


def constant_tables():
    depth, tangent = window_tables()
    pairs = [(0, s, 0) for s in range(2)]
    pairs += [(1, s, 2 * t) for s in range(4) for t in range(2)]
    pairs += [(2, 0, 0)]
    cols = []
    for kind, sa, sb in pairs:
        tile = np.zeros((16, 16, 8, 2, 8))
        for parity in range(2):
            tile[:, :, :, parity, :] = np.einsum(
                "pa,qb->abpq", tangent[kind, sa], tangent[kind, sb + parity]
            )
        cols.append(tile.reshape(256, 128))
    cols.append(np.zeros((256, 128)))
    tangents = np.concatenate(cols, 1)
    picks = np.zeros((2, 3, 2, 16, 10, 8))
    for kind in range(3):
        for b in range(2):
            for f in range(5):
                for i in range(3):
                    for layer in range(5):
                        picks[0, kind, b, f * 3 + i, b * 5 + f, layer] = depth[kind, i, layer]
                        picks[1, kind, b, f * 3 + i, b * 5 + f, 7 - layer] = depth[kind, i, layer]
    return tangents, picks.reshape(2, 96, 80)


def parts_of(count, x):
    parts = []
    for n in range(count):
        part = x.astype(BF16)
        parts.append(part)
        if n < count - 1:
            x = x - part.astype(F32)
    return parts


def dot(a, b):
    return jnp.dot(a, b, preferred_element_type=F32)


def iotas():
    lane = lax.broadcasted_iota(jnp.int32, (8, 128), 1)
    row = lax.broadcasted_iota(jnp.int32, (8, 128), 0)
    return lane, row


def swap(planes, lane, bit, reach):
    keep = (lane & reach) == 0
    out = list(planes)
    for v in range(8):
        if not (v >> bit) & 1:
            w = v | (1 << bit)
            out[v] = jnp.where(keep, planes[v], pltpu.roll(planes[w], reach, 1))
            out[w] = jnp.where(keep, pltpu.roll(planes[v], 128 - reach, 1), planes[w])
    return out


def swaps(planes, lane, reach):
    for bit in (2, 1, 0):
        planes = swap(planes, lane, bit, reach << bit)
    return planes


def cross(x, lane, row):
    odd = row & 1
    low = jnp.where(odd == 0, x, pltpu.roll(x, 1, 0))
    high = jnp.where(odd == 0, pltpu.roll(x, 7, 0), x)
    index = (lane & 7) * 16 + odd * 8 + lax.shift_right_logical(lane, 4)
    return jnp.where(
        (lane & 8) == 0,
        jnp.take_along_axis(low, index, axis=1),
        jnp.take_along_axis(high, index, axis=1),
    )


def turned(planes, dim, lane, row):
    if dim == 1:
        return swaps(planes, lane, 16)
    return [cross(x, lane, row) for x in swaps(planes, lane, 1)]


def turned_back(planes, dim, lane, row):
    if dim == 1:
        return swaps(planes, lane, 16)
    return swaps([cross(x, lane, row) for x in planes], lane, 1)


def row_of(dim, half, block, h):
    return half * 4 + block * 2 + h if dim == 0 else h * 4 + block * 2 + half


def plane_rows(ref, dim, half, base=0):
    return jnp.concatenate(
        [
            jnp.concatenate(
                [ref[pl.ds(base + f * 64 + row_of(dim, half, b, h), 8, stride=8), :] for h in range(2)], 1
            )
            for b in range(2)
            for f in range(5)
        ],
        0,
    )


def section_kernel(
    nz, n_node, n_core,
    x_hbm, send_ref, recv_ref, mig_ref, level_ref, flag_ref, tan_hbm, pick_hbm, lane_hbm, line_hbm,
    out_ref,
    x_ref, turns, left, wide, slabs, got, want_out, want_in, stage_g, stage_x, ghost_ref, moved_ref, peak, peaks,
    cells, rims, plus, minus, change, result, tan_ref, pick_ref, lane_ref, line_ref,
    slab_s, slab_r, want_s, want_r, move_s, move_r, peak_s, peak_r, load_s,
):
    node, core = lax.axis_index("node"), lax.axis_index("cores")
    me = node * n_core + core
    total = n_node * n_core
    ny = n_node // nz
    z, y = node % nz, node // nz
    lane, row = iotas()

    def along(offset):
        other = (me + offset + total) % total
        return (other // n_core, other % n_core)

    groups = [
        [(node, (core + t) % n_core) for t in range(1, n_core)],
        [(y * nz + (z + t) % nz, core) for t in range(1, nz)],
        [(((y + t) % ny) * nz + z, core) for t in range(1, ny)],
    ]
    offsets = [o for o in range(-REACH, REACH + 1) if o != 0]
    partners = [d for group in groups for d in group] + [along(o) for o in offsets]
    barrier = pltpu.get_barrier_semaphore()
    for d in partners:
        pl.semaphore_signal(barrier, inc=1, device_id=d, device_id_type=MESH)
    load_x = pltpu.make_async_copy(x_hbm, x_ref, load_s.at[0])
    load_pick = pltpu.make_async_copy(pick_hbm, pick_ref, load_s.at[1])
    load_tan = pltpu.make_async_copy(tan_hbm, tan_ref, load_s.at[2])
    load_lane = pltpu.make_async_copy(lane_hbm, lane_ref, load_s.at[3])
    load_line = pltpu.make_async_copy(line_hbm, line_ref, load_s.at[4])
    for load in (load_x, load_pick, load_tan, load_lane, load_line):
        load.start()

    def send_peaks(phase):
        base = sum(len(g) for g in groups[:phase])
        copies = [
            pltpu.make_async_remote_copy(
                src_ref=peak.at[phase],
                dst_ref=peaks.at[base + t],
                send_sem=peak_s.at[base + t],
                recv_sem=peak_r.at[base + t],
                device_id=d,
                device_id_type=MESH,
            )
            for t, d in enumerate(groups[phase])
        ]
        for c in copies:
            c.start()
        return copies

    def take_peaks(phase, copies):
        base = sum(len(g) for g in groups[:phase])
        for c in copies:
            c.wait_recv()
        best = peak[phase]
        for t in range(len(copies)):
            best = jnp.maximum(best, peaks[base + t])
        return best

    load_x.wait()
    for f in range(5):
        for c in range(32):
            at = f * 64 + (c // 2 % 8) * 8 + (c // 16) * 4 + c % 2
            turns[pl.ds(at, 2, stride=2), :] = x_ref[f, :, c * 128 : c * 128 + 128]
    top = None
    for v in range(8):
        u = [turns[f * 64 + v * 8 : f * 64 + v * 8 + 8] for f in range(5)]
        inv = 1.0 / u[0]
        vel = [u[1 + i] * inv for i in range(3)]
        kinetic = u[1] * vel[0] + u[2] * vel[1] + u[3] * vel[2]
        pressure = 0.4 * (u[4] - 0.5 * kinetic)
        speed = jnp.maximum(jnp.maximum(jnp.abs(vel[0]), jnp.abs(vel[1])), jnp.abs(vel[2]))
        speed = speed + jnp.sqrt(1.4 * pressure * inv)
        top = speed if v == 0 else jnp.maximum(top, speed)
    scales = [lax.shift_left(jnp.int32(EDGE), level_ref[b]).astype(F32) for b in range(2)]
    rated = top * jnp.where((row & 2) == 0, scales[0], scales[1])
    peak[0, 0:8] = jnp.full((8, 128), jnp.max(top), F32)
    peak[0, 8:16] = jnp.full((8, 128), jnp.max(rated), F32)
    for n, direction in enumerate((1, -1)):
        want = jnp.int32(0)
        for j in range(2):
            source = mig_ref[j]
            want = want + jnp.where(source // 2 == me + direction, source % 2, 0)
        want_out[n] = jnp.full((8, 128), want, jnp.int32).astype(F32)
    pl.semaphore_wait(barrier, len(partners))
    first = send_peaks(0)
    want_copies = [
        pltpu.make_async_remote_copy(
            src_ref=want_out.at[n],
            dst_ref=want_in.at[n],
            send_sem=want_s.at[n],
            recv_sem=want_r.at[n],
            device_id=along(direction),
            device_id_type=MESH,
        )
        for n, direction in enumerate((1, -1))
    ]
    for c in want_copies:
        c.start()
    for f in range(5):
        planes = [turns[f * 64 + v * 8 : f * 64 + v * 8 + 8] for v in range(8)]
        for dim in (1, 2):
            for v, value in enumerate(turned(planes, dim, lane, row)):
                at = dim * 320 + f * 64 + v * 8
                turns[at : at + 8] = value
    load_pick.wait()
    for g in range(6):
        side = g % 2
        parts = parts_of(2, plane_rows(turns, g // 2, side, (g // 2) * 320))
        rows = sum(dot(pick_ref[side], part) for part in parts)
        for n, part in enumerate(parts_of(2, rows)):
            for kind in range(3):
                left[kind, n, g * 32 : g * 32 + 32] = part[kind * 32 : kind * 32 + 32]
    load_tan.wait()
    for tile in range(6):
        kind = 0 if tile == 0 else 1 if tile < 5 else 2
        weights = tan_ref[:, tile * 256 : tile * 256 + 256]
        out = sum(dot(left[kind, n], weights) for n in range(2))
        wide[2 * tile] = out[:, 0:128].reshape(12, 16, 128)
        if tile < 5:
            wide[2 * tile + 1] = out[:, 128:256].reshape(12, 16, 128)
    even = (lane & 8) == 0

    def entry(k, into, at):
        blk, g, kind = send_ref[0, k], send_ref[1, k], send_ref[2, k]
        sa, sb = send_ref[3, k], send_ref[4, k]
        pair = jnp.where(kind == 0, sa % 2, jnp.where(kind == 1, 2 + sa * 2 + sb // 2, 10))
        parity = jnp.where(kind == 2, 0, sb % 2)
        low = wide[pair, g * 2 + blk, 0:8]
        high = wide[pair, g * 2 + blk, 8:16]
        ahead = jnp.where(even, low, pltpu.roll(high, 8, 1))
        behind = jnp.where(even, pltpu.roll(low, 120, 1), high)
        into[at] = jnp.where(jnp.full((8, 128), parity, jnp.int32) == 0, ahead, behind)

    slab_copies = []
    for n, o in enumerate(offsets):
        for m in range(CAP):
            entry((o + REACH) * CAP + m, slabs, n * CAP + m)
        copy = pltpu.make_async_remote_copy(
            src_ref=slabs.at[pl.ds(n * CAP, CAP)],
            dst_ref=got.at[pl.ds((REACH - o) * CAP, CAP)],
            send_sem=slab_s.at[n],
            recv_sem=slab_r.at[n],
            device_id=along(o),
            device_id_type=MESH,
        )
        copy.start()
        slab_copies.append(copy)
    for m in range(CAP):
        entry(REACH * CAP + m, got, REACH * CAP + m)
    peak[1] = take_peaks(0, first)
    second = send_peaks(1)
    for c in want_copies:
        c.wait_recv()
    second_block = [want_in[n] > 0.5 for n in range(2)]
    for n in range(2):
        pick = second_block[n]
        for f in range(5):
            for t in range(4):
                at = f * 64 + t * 16
                one, two = turns[at : at + 8], turns[at + 8 : at + 16]
                one = jnp.where(pick, pltpu.roll(one, 6, 0), one)
                two = jnp.where(pick, two, pltpu.roll(two, 2, 0))
                stage_x[n, f, t] = jnp.where((row & 2) == 0, one, two)
    move_copies = []
    for n, direction in enumerate((-1, 1)):
        for m, (src, dst) in enumerate(
            (
                (stage_x.at[n], moved_ref.at[1 - n]),
                (stage_g.at[n], ghost_ref.at[3 - n]),
            )
        ):
            move_copies.append(
                pltpu.make_async_remote_copy(
                    src_ref=src,
                    dst_ref=dst,
                    send_sem=move_s.at[2 * n + m],
                    recv_sem=move_r.at[2 * n + m],
                    device_id=along(direction),
                    device_id_type=MESH,
                )
            )
    move_copies[0].start()
    move_copies[2].start()
    peak[2] = take_peaks(1, second)
    third = send_peaks(2)
    for c in slab_copies:
        c.wait_recv()
    for g in range(6):
        for qa in range(2):
            pair = []
            for b in range(2):
                at = (b * 6 + g) * 4 + 2 * qa
                one, two = got[recv_ref[at]], got[recv_ref[at + 1]]
                low = jnp.where(even, one, pltpu.roll(two, 8, 1))
                high = jnp.where(even, pltpu.roll(one, 120, 1), two)
                high = jnp.where(row == 7, scales[b], high)
                ghost_ref[b, g, qa, 0:8] = low
                ghost_ref[b, g, qa, 8:16] = high
                pair.append((low, high))
            for n in range(2):
                pick = second_block[n]
                stage_g[n, g, qa, 0:8] = jnp.where(pick, pair[1][0], pair[0][0])
                stage_g[n, g, qa, 8:16] = jnp.where(pick, pair[1][1], pair[0][1])
    move_copies[1].start()
    move_copies[3].start()
    slots = []
    for j in range(2):
        source = mig_ref[j]
        far = jnp.where(source // 2 < me, 2, 3)
        slots.append(jnp.where(source // 2 == me, source % 2, far))
    move_copies[0].wait_recv()
    move_copies[2].wait_recv()
    for f in range(5):
        planes = []
        for v in range(8):
            own = turns[f * 64 + v * 8 : f * 64 + v * 8 + 8]
            down, up = moved_ref[0, f, v // 2], moved_ref[1, f, v // 2]
            for b in range(2):
                away = 6 if b == 0 else 2
                mine = jnp.where(slots[b] == b, own, pltpu.roll(own, away, 0))
                other = jnp.where(slots[b] == 2, down, up)
                if v % 2 != b:
                    other = pltpu.roll(other, away, 0)
                value = jnp.where(slots[b] < 2, mine, other)
                both = value if b == 0 else jnp.where((row & 2) == 0, both, value)
            planes.append(both)
        for a in range(3):
            layout = planes if a == 0 else turned(planes, a, lane, row)
            up, down = (4, 4) if a == 0 else (1, 7)
            for v in range(8):
                cells[a, f, 3 + v] = layout[v]
            for layer in range(3):
                cells[a, f, 2 - layer] = pltpu.roll(layout[7 - layer], up, 0)
                cells[a, f, 11 + layer] = pltpu.roll(layout[layer], down, 0)
    top = take_peaks(2, third)
    fastest = top[0:8]
    step = 0.4 / top[8:16]

    def flux(a, p, u):
        inv = 1.0 / u[0]
        v = [u[1 + i] * inv for i in range(3)]
        kinetic = u[1] * v[0] + u[2] * v[1] + u[3] * v[2]
        pressure = 0.4 * (u[4] - 0.5 * kinetic)
        flow = [u[1 + a]] + [u[1 + i] * v[a] for i in range(3)] + [(u[4] + pressure) * v[a]]
        flow[1 + a] = flow[1 + a] + pressure
        for f in range(5):
            plus[a, f, p] = 0.5 * (flow[f] + fastest * u[f])
            minus[a, f, p] = 0.5 * (flow[f] - fastest * u[f])

    for a in range(3):

        def inner(p, carry):
            flux(a, p, [cells[a, f, p] for f in range(5)])
            return carry

        lax.fori_loop(3, 11, inner, 0, unroll=2)
    move_copies[1].wait_recv()
    move_copies[3].wait_recv()
    for b in range(2):
        for g in range(6):
            for h in range(2):
                base = (g // 2) * 128 + row_of(g // 2, g % 2, b, h)
                rims[pl.ds(base, 8, stride=8), :] = ghost_ref[slots[b], g, h, 0:8]
                rims[pl.ds(base + 64, 8, stride=8), :] = ghost_ref[slots[b], g, h, 8:16]
    factor = step * rims[120:128]
    for a in range(3):
        lower = (row & (4 if a == 0 else 1)) == 0
        for layer in range(3):
            rim = [rims[a * 128 + (f * 3 + layer) * 8 : a * 128 + (f * 3 + layer) * 8 + 8] for f in range(5)]
            low, high = 2 - layer, 11 + layer
            flux(a, low, [jnp.where(lower, rim[f], cells[a, f, low]) for f in range(5)])
            flux(a, high, [jnp.where(lower, cells[a, f, high], rim[f]) for f in range(5)])

        def field(f, carry):
            hat = weno(plus[a, f], 2, False) + weno(minus[a, f], 3, True)
            change[a, f] = hat[1:] - hat[:-1]
            return carry

        lax.fori_loop(0, 5, field, 0)
    for f in range(5):
        second_part = turned_back([change[1, f, v] for v in range(8)], 1, lane, row)
        third_part = turned_back([change[2, f, v] for v in range(8)], 2, lane, row)
        for v in range(8):
            moved = change[0, f, v] + second_part[v] + third_part[v]
            result[f * 64 + v * 8 : f * 64 + v * 8 + 8] = cells[0, f, 3 + v] - factor * moved
    load_lane.wait()
    load_line.wait()
    halves = [plane_rows(result, 0, half) for half in range(2)]
    cubes = jnp.concatenate(
        [halves[half][n * 8 : n * 8 + 8] for n in range(10) for half in range(2)], 0
    )
    smooth = sum(dot(part, lane_ref[...]) for part in parts_of(3, cubes))
    smooth = sum(dot(line_ref[...], part) for part in parts_of(3, smooth))
    for b in range(2):
        kept = jnp.where(flag_ref[b] == 1, smooth[b * 80 : b * 80 + 80], cubes[b * 80 : b * 80 + 80])
        for f in range(5):
            for half in range(2):
                at = f * 16 + half * 8
                for h in range(2):
                    base = f * 64 + row_of(0, half, b, h)
                    result[pl.ds(base, 8, stride=8), :] = kept[at : at + 8, h * 128 : h * 128 + 128]
    for f in range(5):
        for c in range(32):
            at = f * 64 + (c // 2 % 8) * 8 + (c // 16) * 4 + c % 2
            out_ref[f, :, c * 128 : c * 128 + 128] = result[pl.ds(at, 2, stride=2), :]
    for c in first + second + third + want_copies + slab_copies + move_copies:
        c.wait_send()


def weno(values, centres, mirrored):
    half = 0.5 * (values[1:] - values[:-1])
    bend = half[1:] - half[:-1]
    rough = 1e-6 + (13.0 / 3.0) * (bend * bend)
    third = bend * (1.0 / 3.0)
    lo, n = centres, 9
    gl, gr = half[lo - 1 : lo - 1 + n], half[lo : lo + n]
    bl, bc, br = (slice(lo - 2 + t, lo - 2 + t + n) for t in range(3))
    tl = 2.0 * gl + bend[bl]
    tc = gl + gr
    tr = 2.0 * gr - bend[br]
    sl = rough[bl] + tl * tl
    sc = rough[bc] + tc * tc
    sr = rough[br] + tr * tr
    il = pl.reciprocal(sl, approx=True)
    ic = pl.reciprocal(sc, approx=True)
    ir = pl.reciprocal(sr, approx=True)
    wl, wc, wr = il * il, 6.0 * (ic * ic), ir * ir
    if mirrored:
        wl = 3.0 * wl
        cl = third[bl] + gl
        cc = third[bc] + gl
        cr = gr - 2.0 * third[br]
        total = wl * cl + wc * cc + wr * cr
        sign = -1.0
    else:
        wr = 3.0 * wr
        cl = gl + 2.0 * third[bl]
        cc = gr - third[bc]
        cr = gr - third[br]
        total = wl * cl + wc * cc + wr * cr
        sign = 1.0
    share = total * pl.reciprocal(wl + wc + wr, approx=True)
    centre = values[lo : lo + n]
    return centre + share if sign > 0 else centre - share


def solution(mesh):
    n_node, n_core = mesh.shape["node"], mesh.shape["cores"]
    nz = max(1, int(round(n_node**0.5)))
    tangents, picks = constant_tables()
    smoother = predict_table(8) @ np.eye(16)[0::2]
    lane_smoother = np.kron(smoother, smoother).T
    line_smoother = np.kron(np.eye(10), smoother)
    groups = n_core - 1 + nz - 1 + n_node // nz - 1

    def body(block_state, levels, send_table, receive_table, migration, coarsen_flags):
        state = pl.pallas_call(
            functools.partial(section_kernel, nz, n_node, n_core),
            out_shape=jax.ShapeDtypeStruct((5, 2, 4096), F32),
            in_specs=[HB, SM, SM, SM, SM, SM, HB, HB, HB, HB],
            out_specs=VM,
            scratch_shapes=[
                pltpu.VMEM((5, 2, 4096), F32),
                pltpu.VMEM((960, 128), F32),
                pltpu.VMEM((3, 2, 192, 256), BF16),
                pltpu.VMEM((11, 12, 16, 128), F32),
                pltpu.VMEM((SLOTS - CAP, 8, 128), F32),
                pltpu.VMEM((SLOTS, 8, 128), F32),
                pltpu.VMEM((2, 8, 128), F32),
                pltpu.VMEM((2, 8, 128), F32),
                pltpu.VMEM((2, 6, 2, 16, 128), F32),
                pltpu.VMEM((2, 5, 4, 8, 128), F32),
                pltpu.VMEM((4, 6, 2, 16, 128), F32),
                pltpu.VMEM((2, 5, 4, 8, 128), F32),
                pltpu.VMEM((3, 16, 128), F32),
                pltpu.VMEM((groups, 16, 128), F32),
                pltpu.VMEM((3, 5, 14, 8, 128), F32),
                pltpu.VMEM((3 * 16 * 8, 128), F32),
                pltpu.VMEM((3, 5, 14, 8, 128), F32),
                pltpu.VMEM((3, 5, 14, 8, 128), F32),
                pltpu.VMEM((3, 5, 8, 8, 128), F32),
                pltpu.VMEM((320, 128), F32),
                pltpu.VMEM((256, 1536), BF16),
                pltpu.VMEM((2, 96, 80), BF16),
                pltpu.VMEM((256, 256), BF16),
                pltpu.VMEM((160, 160), BF16),
                pltpu.SemaphoreType.DMA((6,)),
                pltpu.SemaphoreType.DMA((6,)),
                pltpu.SemaphoreType.DMA((2,)),
                pltpu.SemaphoreType.DMA((2,)),
                pltpu.SemaphoreType.DMA((4,)),
                pltpu.SemaphoreType.DMA((4,)),
                pltpu.SemaphoreType.DMA((groups,)),
                pltpu.SemaphoreType.DMA((groups,)),
                pltpu.SemaphoreType.DMA((5,)),
            ],
            compiler_params=pltpu.CompilerParams(
                collective_id=0, has_side_effects=True, vmem_limit_bytes=VMEM_BYTES
            ),
            name="section",
        )(
            jnp.transpose(block_state, (1, 0, 2)), send_table, receive_table, migration, levels, coarsen_flags,
            jnp.asarray(tangents, BF16), jnp.asarray(picks, BF16),
            jnp.asarray(lane_smoother, BF16), jnp.asarray(line_smoother, BF16),
        )
        return jnp.transpose(state, (1, 0, 2))

    both = ("node", "cores")
    return jax.shard_map(
        body,
        mesh=mesh,
        in_specs=(P(both, None, None), P(both), P(None, both), P(both), P(both), P(both)),
        out_specs=P(both, None, None),
        check_vma=False,
    )
```

```python
import functools

import jax
import jax.numpy as jnp
import numpy as np
from jax import lax
from jax.experimental import pallas as pl
from jax.experimental.pallas import tpu as pltpu
from jax.sharding import PartitionSpec as P

MESH = pl.DeviceIdType.MESH
F32 = jnp.float32
BF16 = jnp.bfloat16
EDGE = 16
REACH = 3
CAP = 7
VMEM_BYTES = 63 << 20
SLOTS = 49
VM = pl.BlockSpec(memory_space=pltpu.VMEM)
SM = pl.BlockSpec(memory_space=pltpu.SMEM)
HB = pl.BlockSpec(memory_space=pltpu.HBM)


def predict_table(n):
    w = np.zeros((2 * n, n))
    for c in range(n):
        w[2 * c, c] = 1.0
        if c == 0:
            w[1, 0:4] = np.array([5.0, 15.0, -5.0, 1.0]) / 16.0
        elif c == n - 2:
            w[2 * c + 1, n - 4 : n] = np.array([1.0, -5.0, 15.0, 5.0]) / 16.0
        elif c == n - 1:
            w[2 * c + 1, n - 1] = 1.0
        else:
            w[2 * c + 1, c - 1 : c + 3] = np.array([-1.0, 9.0, 9.0, -1.0]) / 16.0
    return w


def window_tables():
    depth = np.zeros((3, 3, 5))
    depth[0, :, 0:3] = np.eye(3)
    depth[1, :, 0:4] = predict_table(8)[0:3, 0:4]
    depth[2, 0, 0] = depth[2, 1, 2] = depth[2, 2, 4] = 1.0
    eye, fine = np.eye(16), predict_table(16)
    tangent = np.zeros((3, 4, 8, 16))
    for s in range(4):
        tangent[0, s] = eye[8 * (s % 2) : 8 * (s % 2) + 8]
        tangent[1, s] = fine[8 * s : 8 * s + 8]
        tangent[2, s] = eye[0::2]
    return depth, tangent


def constant_tables():
    depth, tangent = window_tables()
    pairs = [(0, s, 0) for s in range(2)]
    pairs += [(1, s, 2 * t) for s in range(4) for t in range(2)]
    pairs += [(2, 0, 0)]
    cols = []
    for kind, sa, sb in pairs:
        tile = np.zeros((16, 16, 8, 2, 8))
        for parity in range(2):
            tile[:, :, :, parity, :] = np.einsum(
                "pa,qb->abpq", tangent[kind, sa], tangent[kind, sb + parity]
            )
        cols.append(tile.reshape(256, 128))
    cols.append(np.zeros((256, 128)))
    tangents = np.concatenate(cols, 1)
    picks = np.zeros((2, 3, 2, 16, 10, 8))
    for kind in range(3):
        for b in range(2):
            for f in range(5):
                for i in range(3):
                    for layer in range(5):
                        picks[0, kind, b, f * 3 + i, b * 5 + f, layer] = depth[kind, i, layer]
                        picks[1, kind, b, f * 3 + i, b * 5 + f, 7 - layer] = depth[kind, i, layer]
    return tangents, picks.reshape(2, 96, 80)


def parts_of(count, x):
    parts = []
    for n in range(count):
        part = x.astype(BF16)
        parts.append(part)
        if n < count - 1:
            x = x - part.astype(F32)
    return parts


def dot(a, b):
    return jnp.dot(a, b, preferred_element_type=F32)


def iotas():
    lane = lax.broadcasted_iota(jnp.int32, (8, 128), 1)
    row = lax.broadcasted_iota(jnp.int32, (8, 128), 0)
    return lane, row


def inverse(x):
    guess = pl.reciprocal(x, approx=True)
    return guess * (2.0 - x * guess)


def swap(planes, lane, bit, reach):
    keep = (lane & reach) == 0
    out = list(planes)
    for v in range(8):
        if not (v >> bit) & 1:
            w = v | (1 << bit)
            out[v] = jnp.where(keep, planes[v], pltpu.roll(planes[w], reach, 1))
            out[w] = jnp.where(keep, pltpu.roll(planes[v], 128 - reach, 1), planes[w])
    return out


def swaps(planes, lane, reach):
    for bit in (2, 1, 0):
        planes = swap(planes, lane, bit, reach << bit)
    return planes


def cross(x, lane, row):
    odd = row & 1
    low = jnp.where(odd == 0, x, pltpu.roll(x, 1, 0))
    high = jnp.where(odd == 0, pltpu.roll(x, 7, 0), x)
    index = (lane & 7) * 16 + odd * 8 + lax.shift_right_logical(lane, 4)
    return jnp.where(
        (lane & 8) == 0,
        jnp.take_along_axis(low, index, axis=1),
        jnp.take_along_axis(high, index, axis=1),
    )


def turned(planes, dim, lane, row):
    if dim == 1:
        return swaps(planes, lane, 16)
    return [cross(x, lane, row) for x in swaps(planes, lane, 1)]


def turned_back(planes, dim, lane, row):
    if dim == 1:
        return swaps(planes, lane, 16)
    return swaps([cross(x, lane, row) for x in planes], lane, 1)


def row_of(dim, half, block, h):
    return half * 4 + block * 2 + h if dim == 0 else h * 4 + block * 2 + half


def plane_rows(ref, dim, half, base=0):
    return jnp.concatenate(
        [
            jnp.concatenate(
                [ref[pl.ds(base + f * 64 + row_of(dim, half, b, h), 8, stride=8), :] for h in range(2)], 1
            )
            for b in range(2)
            for f in range(5)
        ],
        0,
    )


def section_kernel(
    nz, n_node, n_core,
    x_hbm, send_hbm, recv_hbm, mig_hbm, level_hbm, flag_hbm, tan_hbm, pick_hbm, lane_hbm, line_hbm,
    out_ref,
    x_ref, turns, left, wide, slabs, got, want_out, want_in, stage_g, stage_x, ghosts, moved_ref, peak, peaks,
    cells, rims, flows, change, result, tan_ref, pick_ref, lane_ref, line_ref,
    send_ref, recv_ref, mig_ref, level_ref, flag_ref,
    slab_s, slab_r, want_s, want_r, move_s, move_r, peak_s, peak_r, load_s,
):
    node, core = lax.axis_index("node"), lax.axis_index("cores")
    me = node * n_core + core
    total = n_node * n_core
    ny = n_node // nz
    z, y = node % nz, node // nz
    lane, row = iotas()

    def along(offset):
        other = (me + offset + total) % total
        return (other // n_core, other % n_core)

    def around(count):
        return sorted(range(1, count), key=lambda t: (-min(t, count - t), t))

    groups = [
        [(node, (core + t) % n_core) for t in around(n_core)],
        [(y * nz + (z + t) % nz, core) for t in around(nz)],
        [(((y + t) % ny) * nz + z, core) for t in around(ny)],
    ]
    offsets = [o for o in range(-REACH, REACH + 1) if o != 0]
    partners = [d for group in groups for d in group] + [along(o) for o in offsets]
    barrier = pltpu.get_barrier_semaphore()
    for d in partners:
        pl.semaphore_signal(barrier, inc=1, device_id=d, device_id_type=MESH)
    (load_x, load_level, load_mig, load_pick, load_send, load_tan, load_recv, load_flag, load_lane, load_line) = loads = [
        pltpu.make_async_copy(source, target, load_s.at[n])
        for n, (source, target) in enumerate(
            (
                (x_hbm, x_ref),
                (level_hbm, level_ref),
                (mig_hbm, mig_ref),
                (pick_hbm, pick_ref),
                (send_hbm, send_ref),
                (tan_hbm, tan_ref),
                (recv_hbm, recv_ref),
                (flag_hbm, flag_ref),
                (lane_hbm, lane_ref),
                (line_hbm, line_ref),
            )
        )
    ]
    for load in loads:
        load.start()

    firsts = [sum(len(g) for g in groups[:phase]) for phase in range(4)]

    def send_peaks(phase):
        for t, d in enumerate(groups[phase]):
            pltpu.make_async_remote_copy(
                src_ref=peak.at[phase],
                dst_ref=peaks.at[firsts[phase] + t],
                send_sem=peak_s.at[phase],
                recv_sem=peak_r.at[phase],
                device_id=d,
                device_id_type=MESH,
            ).start()

    def all_peaks(phase):
        slots = peaks.at[pl.ds(firsts[phase], len(groups[phase]))]
        return pltpu.make_async_remote_copy(
            src_ref=slots,
            dst_ref=slots,
            send_sem=peak_s.at[phase],
            recv_sem=peak_r.at[phase],
            device_id=groups[phase][0],
            device_id_type=MESH,
        )

    def take_peaks(phase):
        all_peaks(phase).wait_recv()
        best = peak[phase]
        for t in range(len(groups[phase])):
            best = jnp.maximum(best, peaks[firsts[phase] + t])
        return best

    load_x.wait()
    for f in range(5):
        for c in range(32):
            at = f * 64 + (c // 2 % 8) * 8 + (c // 16) * 4 + c % 2
            turns[pl.ds(at, 2, stride=2), :] = x_ref[f, :, c * 128 : c * 128 + 128]
    top = None
    for v in range(8):
        u = [turns[f * 64 + v * 8 : f * 64 + v * 8 + 8] for f in range(5)]
        inv = inverse(u[0])
        vel = [u[1 + i] * inv for i in range(3)]
        kinetic = u[1] * vel[0] + u[2] * vel[1] + u[3] * vel[2]
        pressure = 0.4 * (u[4] - 0.5 * kinetic)
        speed = jnp.maximum(jnp.maximum(jnp.abs(vel[0]), jnp.abs(vel[1])), jnp.abs(vel[2]))
        speed = speed + jnp.sqrt(1.4 * pressure * inv)
        top = speed if v == 0 else jnp.maximum(top, speed)
    load_level.wait()
    load_mig.wait()
    scales = [lax.shift_left(jnp.int32(EDGE), level_ref[b]).astype(F32) for b in range(2)]
    rated = top * jnp.where((row & 2) == 0, scales[0], scales[1])
    upper = (lane[0:1] & 64) != 0
    peak[0] = jnp.where(upper, jnp.max(rated), jnp.max(top))
    for n, direction in enumerate((1, -1)):
        want = jnp.int32(0)
        for j in range(2):
            source = mig_ref[j]
            want = want + jnp.where(source // 2 == me + direction, source % 2, 0)
        want_out[n] = jnp.full((8, 128), want, jnp.int32).astype(F32)
    pl.semaphore_wait(barrier, len(partners))
    send_peaks(0)
    want_copies = [
        pltpu.make_async_remote_copy(
            src_ref=want_out.at[n],
            dst_ref=want_in.at[n],
            send_sem=want_s.at[n],
            recv_sem=want_r.at[n],
            device_id=along(direction),
            device_id_type=MESH,
        )
        for n, direction in enumerate((1, -1))
    ]
    for c in want_copies:
        c.start()
    for f in range(5):
        planes = [turns[f * 64 + v * 8 : f * 64 + v * 8 + 8] for v in range(8)]
        for dim in (1, 2):
            for v, value in enumerate(turned(planes, dim, lane, row)):
                at = dim * 320 + f * 64 + v * 8
                turns[at : at + 8] = value
    load_pick.wait()
    for g in range(6):
        side = g % 2
        parts = parts_of(2, plane_rows(turns, g // 2, side, (g // 2) * 320))
        rows = sum(dot(pick_ref[side], part) for part in parts)
        for n, part in enumerate(parts_of(2, rows)):
            for kind in range(3):
                left[kind, n, g * 32 : g * 32 + 32] = part[kind * 32 : kind * 32 + 32]
    load_tan.wait()
    for tile in range(6):
        kind = 0 if tile == 0 else 1 if tile < 5 else 2
        weights = tan_ref[:, tile * 256 : tile * 256 + 256]
        out = sum(dot(left[kind, n], weights) for n in range(2))
        wide[2 * tile] = out[:, 0:128].reshape(12, 16, 128)
        if tile < 5:
            wide[2 * tile + 1] = out[:, 128:256].reshape(12, 16, 128)
    even = (lane & 8) == 0
    load_send.wait()

    def entry(k, into, at):
        blk, g, kind = send_ref[0, k], send_ref[1, k], send_ref[2, k]
        sa, sb = send_ref[3, k], send_ref[4, k]
        pair = jnp.where(kind == 0, sa % 2, jnp.where(kind == 1, 2 + sa * 2 + sb // 2, 10))
        parity = jnp.where(kind == 2, 0, sb % 2)
        low = wide[pair, g * 2 + blk, 0:8]
        high = wide[pair, g * 2 + blk, 8:16]
        ahead = jnp.where(even, low, pltpu.roll(high, 8, 1))
        behind = jnp.where(even, pltpu.roll(low, 120, 1), high)
        into[at] = jnp.where(jnp.full((8, 128), parity, jnp.int32) == 0, ahead, behind)

    slab_copies = []
    for n, o in enumerate(offsets):
        for m in range(CAP):
            entry((o + REACH) * CAP + m, slabs, n * CAP + m)
        copy = pltpu.make_async_remote_copy(
            src_ref=slabs.at[pl.ds(n * CAP, CAP)],
            dst_ref=got.at[pl.ds((REACH - o) * CAP, CAP)],
            send_sem=slab_s.at[n],
            recv_sem=slab_r.at[n],
            device_id=along(o),
            device_id_type=MESH,
        )
        copy.start()
        slab_copies.append(copy)
    for m in range(CAP):
        entry(REACH * CAP + m, got, REACH * CAP + m)
    load_recv.wait()
    load_flag.wait()
    peak[1] = take_peaks(0)
    send_peaks(1)
    peak[2] = take_peaks(1)
    send_peaks(2)
    for c in want_copies:
        c.wait_recv()
    second_block = [want_in[n] > 0.5 for n in range(2)]
    for n in range(2):
        pick = second_block[n]
        for f in range(5):
            for t in range(4):
                at = f * 64 + t * 16
                one, two = turns[at : at + 8], turns[at + 8 : at + 16]
                one = jnp.where(pick, pltpu.roll(one, 6, 0), one)
                two = jnp.where(pick, two, pltpu.roll(two, 2, 0))
                stage_x[n, f, t] = jnp.where((row & 2) == 0, one, two)
    def move(n, piece, source, target):
        copy = pltpu.make_async_remote_copy(
            src_ref=source,
            dst_ref=target,
            send_sem=move_s.at[n, piece],
            recv_sem=move_r.at[n, piece],
            device_id=along((-1, 1)[n]),
            device_id_type=MESH,
        )
        copy.start()
        return copy

    state_copies = [move(n, 3, stage_x.at[n], moved_ref.at[1 - n]) for n in range(2)]
    for c in slab_copies:
        c.wait_recv()
    rim_copies = []
    for a in range(3):
        for side in range(2):
            g = 2 * a + side
            for qa in range(2):
                pair = []
                for b in range(2):
                    at = (b * 6 + g) * 4 + 2 * qa
                    one, two = got[recv_ref[at]], got[recv_ref[at + 1]]
                    low = jnp.where(even, one, pltpu.roll(two, 8, 1))
                    high = jnp.where(even, pltpu.roll(one, 120, 1), two)
                    high = jnp.where(row == 7, scales[b], high)
                    ghosts[a][b, side, qa, 0:8] = low
                    ghosts[a][b, side, qa, 8:16] = high
                    pair.append((low, high))
                for n in range(2):
                    pick = second_block[n]
                    stage_g[a, n, side, qa, 0:8] = jnp.where(pick, pair[1][0], pair[0][0])
                    stage_g[a, n, side, qa, 8:16] = jnp.where(pick, pair[1][1], pair[0][1])
        rim_copies.append([move(n, a, stage_g.at[a, n], ghosts[a].at[3 - n]) for n in range(2)])
    slots = []
    for j in range(2):
        source = mig_ref[j]
        far = jnp.where(source // 2 < me, 2, 3)
        slots.append(jnp.where(source // 2 == me, source % 2, far))
    for c in state_copies:
        c.wait_recv()
    for f in range(5):
        planes = []
        for v in range(8):
            own = turns[f * 64 + v * 8 : f * 64 + v * 8 + 8]
            down, up = moved_ref[0, f, v // 2], moved_ref[1, f, v // 2]
            for b in range(2):
                away = 6 if b == 0 else 2
                mine = jnp.where(slots[b] == b, own, pltpu.roll(own, away, 0))
                other = jnp.where(slots[b] == 2, down, up)
                if v % 2 != b:
                    other = pltpu.roll(other, away, 0)
                value = jnp.where(slots[b] < 2, mine, other)
                both = value if b == 0 else jnp.where((row & 2) == 0, both, value)
            planes.append(both)
        for a in range(3):
            layout = planes if a == 0 else turned(planes, a, lane, row)
            up, down = (4, 4) if a == 0 else (1, 7)
            for v in range(8):
                cells[a, f, 3 + v] = layout[v]
            for layer in range(3):
                cells[a, f, 2 - layer] = pltpu.roll(layout[7 - layer], up, 0)
                cells[a, f, 11 + layer] = pltpu.roll(layout[layer], down, 0)
    def flux(a, p, u):
        inv = inverse(u[0])
        v = [u[1 + i] * inv for i in range(3)]
        kinetic = u[1] * v[0] + u[2] * v[1] + u[3] * v[2]
        pressure = 0.4 * (u[4] - 0.5 * kinetic)
        flow = [u[1 + a]] + [u[1 + i] * v[a] for i in range(3)] + [(u[4] + pressure) * v[a]]
        flow[1 + a] = flow[1 + a] + pressure
        for f in range(5):
            flows[a, f, p] = 0.5 * flow[f]

    for a in range(3):

        def inner(p, carry):
            flux(a, p, [cells[a, f, p] for f in range(5)])
            return carry

        lax.fori_loop(3, 11, inner, 0, unroll=4)
    top = take_peaks(2)
    half_fastest = 0.5 * jnp.max(jnp.where(upper, 0.0, top))
    step = 0.4 / jnp.full((8, 128), jnp.max(jnp.where(upper, top, 0.0)), F32)
    for a in range(3):
        for c in rim_copies[a]:
            c.wait_recv()
        for b in range(2):
            for side in range(2):
                for h in range(2):
                    base = a * 128 + row_of(a, side, b, h)
                    rims[pl.ds(base, 8, stride=8), :] = ghosts[a][slots[b], side, h, 0:8]
                    rims[pl.ds(base + 64, 8, stride=8), :] = ghosts[a][slots[b], side, h, 8:16]
        if a == 0:
            factor = step * rims[120:128]
        lower = (row & (4 if a == 0 else 1)) == 0
        for layer in range(3):
            rim = [rims[a * 128 + (f * 3 + layer) * 8 : a * 128 + (f * 3 + layer) * 8 + 8] for f in range(5)]
            low, high = 2 - layer, 11 + layer
            below = [jnp.where(lower, rim[f], cells[a, f, low]) for f in range(5)]
            above = [jnp.where(lower, cells[a, f, high], rim[f]) for f in range(5)]
            for f in range(5):
                cells[a, f, low] = below[f]
                cells[a, f, high] = above[f]
            flux(a, low, below)
            flux(a, high, above)

        def field(f, carry):
            flow, spread = flows[a, f], half_fastest * cells[a, f]
            hat = weno(flow + spread, 2, False) + weno(flow - spread, 3, True)
            change[a, f] = hat[1:] - hat[:-1]
            return carry

        lax.fori_loop(0, 5, field, 0)
    for f in range(5):
        second_part = turned_back([change[1, f, v] for v in range(8)], 1, lane, row)
        third_part = turned_back([change[2, f, v] for v in range(8)], 2, lane, row)
        for v in range(8):
            moved = change[0, f, v] + second_part[v] + third_part[v]
            result[f * 64 + v * 8 : f * 64 + v * 8 + 8] = cells[0, f, 3 + v] - factor * moved
    load_lane.wait()
    load_line.wait()
    halves = [plane_rows(result, 0, half) for half in range(2)]
    cubes = jnp.concatenate(
        [halves[half][n * 8 : n * 8 + 8] for n in range(10) for half in range(2)], 0
    )
    smooth = sum(dot(part, lane_ref[...]) for part in parts_of(3, cubes))
    smooth = sum(dot(line_ref[...], part) for part in parts_of(3, smooth))
    for b in range(2):
        kept = jnp.where(flag_ref[b] == 1, smooth[b * 80 : b * 80 + 80], cubes[b * 80 : b * 80 + 80])
        for f in range(5):
            for half in range(2):
                at = f * 16 + half * 8
                for h in range(2):
                    base = f * 64 + row_of(0, half, b, h)
                    result[pl.ds(base, 8, stride=8), :] = kept[at : at + 8, h * 128 : h * 128 + 128]
    for f in range(5):
        for c in range(32):
            at = f * 64 + (c // 2 % 8) * 8 + (c // 16) * 4 + c % 2
            out_ref[f, :, c * 128 : c * 128 + 128] = result[pl.ds(at, 2, stride=2), :]
    for phase in range(3):
        all_peaks(phase).wait_send()
    for c in want_copies + slab_copies + state_copies + [c for pair in rim_copies for c in pair]:
        c.wait_send()


def weno(values, centres, mirrored):
    half = 0.5 * (values[1:] - values[:-1])
    bend = half[1:] - half[:-1]
    rough = 1e-6 + (13.0 / 3.0) * (bend * bend)
    third = bend * (1.0 / 3.0)
    lo, n = centres, 9
    gl, gr = half[lo - 1 : lo - 1 + n], half[lo : lo + n]
    bl, bc, br = (slice(lo - 2 + t, lo - 2 + t + n) for t in range(3))
    tl = 2.0 * gl + bend[bl]
    tc = gl + gr
    tr = 2.0 * gr - bend[br]
    sl = rough[bl] + tl * tl
    sc = rough[bc] + tc * tc
    sr = rough[br] + tr * tr
    il = pl.reciprocal(sl, approx=True)
    ic = pl.reciprocal(sc, approx=True)
    ir = pl.reciprocal(sr, approx=True)
    wl, wc, wr = il * il, 6.0 * (ic * ic), ir * ir
    if mirrored:
        wl = 3.0 * wl
        cl = third[bl] + gl
        cc = third[bc] + gl
        cr = gr - 2.0 * third[br]
        total = wl * cl + wc * cc + wr * cr
        sign = -1.0
    else:
        wr = 3.0 * wr
        cl = gl + 2.0 * third[bl]
        cc = gr - third[bc]
        cr = gr - third[br]
        total = wl * cl + wc * cc + wr * cr
        sign = 1.0
    share = total * pl.reciprocal(wl + wc + wr, approx=True)
    centre = values[lo : lo + n]
    return centre + share if sign > 0 else centre - share


def solution(mesh):
    n_node, n_core = mesh.shape["node"], mesh.shape["cores"]
    nz = max(1, int(round(n_node**0.5)))
    tangents, picks = constant_tables()
    smoother = predict_table(8) @ np.eye(16)[0::2]
    lane_smoother = np.kron(smoother, smoother).T
    line_smoother = np.kron(np.eye(10), smoother)
    groups = n_core - 1 + nz - 1 + n_node // nz - 1

    def body(block_state, levels, send_table, receive_table, migration, coarsen_flags):
        state = pl.pallas_call(
            functools.partial(section_kernel, nz, n_node, n_core),
            out_shape=jax.ShapeDtypeStruct((5, 2, 4096), F32),
            in_specs=[HB] * 10,
            out_specs=VM,
            scratch_shapes=[
                pltpu.VMEM((5, 2, 4096), F32),
                pltpu.VMEM((960, 128), F32),
                pltpu.VMEM((3, 2, 192, 256), BF16),
                pltpu.VMEM((11, 12, 16, 128), F32),
                pltpu.VMEM((SLOTS - CAP, 8, 128), F32),
                pltpu.VMEM((SLOTS, 8, 128), F32),
                pltpu.VMEM((2, 8, 128), F32),
                pltpu.VMEM((2, 8, 128), F32),
                pltpu.VMEM((3, 2, 2, 2, 16, 128), F32),
                pltpu.VMEM((2, 5, 4, 8, 128), F32),
                [pltpu.VMEM((4, 2, 2, 16, 128), F32)] * 3,
                pltpu.VMEM((2, 5, 4, 8, 128), F32),
                pltpu.VMEM((3, 1, 128), F32),
                pltpu.VMEM((groups, 1, 128), F32),
                pltpu.VMEM((3, 5, 14, 8, 128), F32),
                pltpu.VMEM((3 * 16 * 8, 128), F32),
                pltpu.VMEM((3, 5, 14, 8, 128), F32),
                pltpu.VMEM((3, 5, 8, 8, 128), F32),
                pltpu.VMEM((320, 128), F32),
                pltpu.VMEM((256, 1536), BF16),
                pltpu.VMEM((2, 96, 80), BF16),
                pltpu.VMEM((256, 256), BF16),
                pltpu.VMEM((160, 160), BF16),
                pltpu.SMEM((5, SLOTS), jnp.int32),
                pltpu.SMEM((48,), jnp.int32),
                pltpu.SMEM((2,), jnp.int32),
                pltpu.SMEM((2,), jnp.int32),
                pltpu.SMEM((2,), jnp.int32),
                pltpu.SemaphoreType.DMA((6,)),
                pltpu.SemaphoreType.DMA((6,)),
                pltpu.SemaphoreType.DMA((2,)),
                pltpu.SemaphoreType.DMA((2,)),
                pltpu.SemaphoreType.DMA((2, 4)),
                pltpu.SemaphoreType.DMA((2, 4)),
                pltpu.SemaphoreType.DMA((3,)),
                pltpu.SemaphoreType.DMA((3,)),
                pltpu.SemaphoreType.DMA((10,)),
            ],
            compiler_params=pltpu.CompilerParams(
                collective_id=0, has_side_effects=True, vmem_limit_bytes=VMEM_BYTES
            ),
            name="section",
        )(
            jnp.transpose(block_state, (1, 0, 2)), send_table, receive_table, migration, levels, coarsen_flags,
            jnp.asarray(tangents, BF16), jnp.asarray(picks, BF16),
            jnp.asarray(lane_smoother, BF16), jnp.asarray(line_smoother, BF16),
        )
        return jnp.transpose(state, (1, 0, 2))

    both = ("node", "cores")
    return jax.shard_map(
        body,
        mesh=mesh,
        in_specs=(P(both, None, None), P(both), P(None, both), P(both), P(both), P(both)),
        out_specs=P(both, None, None),
        check_vma=False,
    )
```

```python
import functools

import jax
import jax.numpy as jnp
import numpy as np
from jax import lax
from jax.experimental import pallas as pl
from jax.experimental.pallas import tpu as pltpu
from jax.sharding import PartitionSpec as P

MESH = pl.DeviceIdType.MESH
F32 = jnp.float32
BF16 = jnp.bfloat16
EDGE = 16
REACH = 3
CAP = 7
VMEM_BYTES = 63 << 20
SLOTS = 49
VM = pl.BlockSpec(memory_space=pltpu.VMEM)
SM = pl.BlockSpec(memory_space=pltpu.SMEM)
HB = pl.BlockSpec(memory_space=pltpu.HBM)


def predict_table(n):
    w = np.zeros((2 * n, n))
    for c in range(n):
        w[2 * c, c] = 1.0
        if c == 0:
            w[1, 0:4] = np.array([5.0, 15.0, -5.0, 1.0]) / 16.0
        elif c == n - 2:
            w[2 * c + 1, n - 4 : n] = np.array([1.0, -5.0, 15.0, 5.0]) / 16.0
        elif c == n - 1:
            w[2 * c + 1, n - 1] = 1.0
        else:
            w[2 * c + 1, c - 1 : c + 3] = np.array([-1.0, 9.0, 9.0, -1.0]) / 16.0
    return w


def window_tables():
    depth = np.zeros((3, 3, 5))
    depth[0, :, 0:3] = np.eye(3)
    depth[1, :, 0:4] = predict_table(8)[0:3, 0:4]
    depth[2, 0, 0] = depth[2, 1, 2] = depth[2, 2, 4] = 1.0
    eye, fine = np.eye(16), predict_table(16)
    tangent = np.zeros((3, 4, 8, 16))
    for s in range(4):
        tangent[0, s] = eye[8 * (s % 2) : 8 * (s % 2) + 8]
        tangent[1, s] = fine[8 * s : 8 * s + 8]
        tangent[2, s] = eye[0::2]
    return depth, tangent


def constant_tables():
    depth, tangent = window_tables()
    pairs = [(0, s, 0) for s in range(2)]
    pairs += [(1, s, 2 * t) for s in range(4) for t in range(2)]
    pairs += [(2, 0, 0)]
    cols = []
    for kind, sa, sb in pairs:
        tile = np.zeros((16, 16, 8, 2, 8))
        for parity in range(2):
            tile[:, :, :, parity, :] = np.einsum(
                "pa,qb->abpq", tangent[kind, sa], tangent[kind, sb + parity]
            )
        cols.append(tile.reshape(256, 128))
    cols.append(np.zeros((256, 128)))
    tangents = np.concatenate(cols, 1)
    picks = np.zeros((2, 3, 2, 16, 10, 8))
    for kind in range(3):
        for b in range(2):
            for f in range(5):
                for i in range(3):
                    for layer in range(5):
                        picks[0, kind, b, f * 3 + i, b * 5 + f, layer] = depth[kind, i, layer]
                        picks[1, kind, b, f * 3 + i, b * 5 + f, 7 - layer] = depth[kind, i, layer]
    return tangents, picks.reshape(2, 96, 80)


def parts_of(count, x):
    parts = []
    for n in range(count):
        part = x.astype(BF16)
        parts.append(part)
        if n < count - 1:
            x = x - part.astype(F32)
    return parts


def dot(a, b):
    return jnp.dot(a, b, preferred_element_type=F32)


def iotas():
    lane = lax.broadcasted_iota(jnp.int32, (8, 128), 1)
    row = lax.broadcasted_iota(jnp.int32, (8, 128), 0)
    return lane, row


def inverse(x):
    guess = pl.reciprocal(x, approx=True)
    return guess * (2.0 - x * guess)


def swap(planes, lane, bit, reach):
    keep = (lane & reach) == 0
    out = list(planes)
    for v in range(8):
        if not (v >> bit) & 1:
            w = v | (1 << bit)
            out[v] = jnp.where(keep, planes[v], pltpu.roll(planes[w], reach, 1))
            out[w] = jnp.where(keep, pltpu.roll(planes[v], 128 - reach, 1), planes[w])
    return out


def swaps(planes, lane, reach):
    for bit in (2, 1, 0):
        planes = swap(planes, lane, bit, reach << bit)
    return planes


def cross(x, lane, row):
    odd = row & 1
    low = jnp.where(odd == 0, x, pltpu.roll(x, 1, 0))
    high = jnp.where(odd == 0, pltpu.roll(x, 7, 0), x)
    index = (lane & 7) * 16 + odd * 8 + lax.shift_right_logical(lane, 4)
    return jnp.where(
        (lane & 8) == 0,
        jnp.take_along_axis(low, index, axis=1),
        jnp.take_along_axis(high, index, axis=1),
    )


def turned(planes, dim, lane, row):
    if dim == 1:
        return swaps(planes, lane, 16)
    return [cross(x, lane, row) for x in swaps(planes, lane, 1)]


def turned_back(planes, dim, lane, row):
    if dim == 1:
        return swaps(planes, lane, 16)
    return swaps([cross(x, lane, row) for x in planes], lane, 1)


def row_of(dim, half, block, h):
    return half * 4 + block * 2 + h if dim == 0 else h * 4 + block * 2 + half


def plane_rows(ref, dim, half, base=0):
    return jnp.concatenate(
        [
            jnp.concatenate(
                [ref[pl.ds(base + f * 64 + row_of(dim, half, b, h), 8, stride=8), :] for h in range(2)], 1
            )
            for b in range(2)
            for f in range(5)
        ],
        0,
    )


def section_kernel(
    nz, n_node, n_core,
    x_hbm, send_hbm, recv_hbm, mig_hbm, level_hbm, flag_hbm, tan_hbm, pick_hbm, lane_hbm, line_hbm,
    out_ref,
    x_ref, turns, left, wide, slabs, got, want_out, want_in, stage_g, stage_x, ghosts, moved_ref, peak, peaks,
    cells, rims, flows, change, result, tan_ref, pick_ref, lane_ref, line_ref,
    send_ref, recv_ref, mig_ref, level_ref, flag_ref,
    slab_s, slab_r, want_s, want_r, move_s, move_r, peak_s, peak_r, load_s,
):
    node, core = lax.axis_index("node"), lax.axis_index("cores")
    me = node * n_core + core
    total = n_node * n_core
    ny = n_node // nz
    z, y = node % nz, node // nz
    lane, row = iotas()

    def along(offset):
        other = (me + offset + total) % total
        return (other // n_core, other % n_core)

    def around(count):
        return sorted(range(1, count), key=lambda t: (-min(t, count - t), t))

    groups = [
        [(node, (core + t) % n_core) for t in around(n_core)],
        [(y * nz + (z + t) % nz, core) for t in around(nz)],
        [(((y + t) % ny) * nz + z, core) for t in around(ny)],
    ]
    offsets = [side * o for o in range(REACH, 0, -1) for side in (-1, 1)]
    partners = [d for group in groups for d in group] + [along(o) for o in offsets]
    barrier = pltpu.get_barrier_semaphore()
    for d in partners:
        pl.semaphore_signal(barrier, inc=1, device_id=d, device_id_type=MESH)
    (load_x, load_level, load_mig, load_pick, load_send, load_tan, load_recv, load_flag, load_lane, load_line) = loads = [
        pltpu.make_async_copy(source, target, load_s.at[n])
        for n, (source, target) in enumerate(
            (
                (x_hbm, x_ref),
                (level_hbm, level_ref),
                (mig_hbm, mig_ref),
                (pick_hbm, pick_ref),
                (send_hbm, send_ref),
                (tan_hbm, tan_ref),
                (recv_hbm, recv_ref),
                (flag_hbm, flag_ref),
                (lane_hbm, lane_ref),
                (line_hbm, line_ref),
            )
        )
    ]
    for load in loads:
        load.start()

    firsts = [sum(len(g) for g in groups[:phase]) for phase in range(4)]

    def send_peaks(phase):
        for t, d in enumerate(groups[phase]):
            pltpu.make_async_remote_copy(
                src_ref=peak.at[phase],
                dst_ref=peaks.at[firsts[phase] + t],
                send_sem=peak_s.at[phase],
                recv_sem=peak_r.at[phase],
                device_id=d,
                device_id_type=MESH,
            ).start()

    def all_peaks(phase):
        slots = peaks.at[pl.ds(firsts[phase], len(groups[phase]))]
        return pltpu.make_async_remote_copy(
            src_ref=slots,
            dst_ref=slots,
            send_sem=peak_s.at[phase],
            recv_sem=peak_r.at[phase],
            device_id=groups[phase][0],
            device_id_type=MESH,
        )

    def take_peaks(phase):
        all_peaks(phase).wait_recv()
        best = peak[phase]
        for t in range(len(groups[phase])):
            best = jnp.maximum(best, peaks[firsts[phase] + t])
        return best

    load_x.wait()
    for f in range(5):
        for c in range(32):
            at = f * 64 + (c // 2 % 8) * 8 + (c // 16) * 4 + c % 2
            turns[pl.ds(at, 2, stride=2), :] = x_ref[f, :, c * 128 : c * 128 + 128]
    top = None
    for v in range(8):
        u = [turns[f * 64 + v * 8 : f * 64 + v * 8 + 8] for f in range(5)]
        inv = inverse(u[0])
        vel = [u[1 + i] * inv for i in range(3)]
        kinetic = u[1] * vel[0] + u[2] * vel[1] + u[3] * vel[2]
        pressure = 0.4 * (u[4] - 0.5 * kinetic)
        speed = jnp.maximum(jnp.maximum(jnp.abs(vel[0]), jnp.abs(vel[1])), jnp.abs(vel[2]))
        speed = speed + jnp.sqrt(1.4 * pressure * inv)
        top = speed if v == 0 else jnp.maximum(top, speed)
    load_level.wait()
    load_mig.wait()
    scales = [lax.shift_left(jnp.int32(EDGE), level_ref[b]).astype(F32) for b in range(2)]
    rated = top * jnp.where((row & 2) == 0, scales[0], scales[1])
    upper = (lane[0:1] & 64) != 0
    peak[0] = jnp.where(upper, jnp.max(rated), jnp.max(top))
    for n, direction in enumerate((1, -1)):
        want = jnp.int32(0)
        for j in range(2):
            source = mig_ref[j]
            want = want + jnp.where(source // 2 == me + direction, source % 2, 0)
        want_out[n] = jnp.full((8, 128), want, jnp.int32).astype(F32)
    pl.semaphore_wait(barrier, len(partners))
    send_peaks(0)
    want_copies = [
        pltpu.make_async_remote_copy(
            src_ref=want_out.at[n],
            dst_ref=want_in.at[n],
            send_sem=want_s.at[n],
            recv_sem=want_r.at[n],
            device_id=along(direction),
            device_id_type=MESH,
        )
        for n, direction in enumerate((1, -1))
    ]
    for c in want_copies:
        c.start()
    for f in range(5):
        planes = [turns[f * 64 + v * 8 : f * 64 + v * 8 + 8] for v in range(8)]
        for dim in (1, 2):
            for v, value in enumerate(turned(planes, dim, lane, row)):
                at = dim * 320 + f * 64 + v * 8
                turns[at : at + 8] = value
    load_pick.wait()
    for g in range(6):
        side = g % 2
        parts = parts_of(2, plane_rows(turns, g // 2, side, (g // 2) * 320))
        rows = sum(dot(pick_ref[side], part) for part in parts)
        for n, part in enumerate(parts_of(2, rows)):
            for kind in range(3):
                left[kind, n, g * 32 : g * 32 + 32] = part[kind * 32 : kind * 32 + 32]
    load_tan.wait()
    for tile in range(6):
        kind = 0 if tile == 0 else 1 if tile < 5 else 2
        weights = tan_ref[:, tile * 256 : tile * 256 + 256]
        out = sum(dot(left[kind, n], weights) for n in range(2))
        wide[2 * tile] = out[:, 0:128].reshape(12, 16, 128)
        if tile < 5:
            wide[2 * tile + 1] = out[:, 128:256].reshape(12, 16, 128)
    even = (lane & 8) == 0
    load_send.wait()

    def entry(k, into, at):
        blk, g, kind = send_ref[0, k], send_ref[1, k], send_ref[2, k]
        sa, sb = send_ref[3, k], send_ref[4, k]
        pair = jnp.where(kind == 0, sa % 2, jnp.where(kind == 1, 2 + sa * 2 + sb // 2, 10))
        parity = jnp.where(kind == 2, 0, sb % 2)
        low = wide[pair, g * 2 + blk, 0:8]
        high = wide[pair, g * 2 + blk, 8:16]
        ahead = jnp.where(even, low, pltpu.roll(high, 8, 1))
        behind = jnp.where(even, pltpu.roll(low, 120, 1), high)
        into[at] = jnp.where(jnp.full((8, 128), parity, jnp.int32) == 0, ahead, behind)

    slab_copies = []
    for n, o in enumerate(offsets):
        for m in range(CAP):
            entry((o + REACH) * CAP + m, slabs, n * CAP + m)
        copy = pltpu.make_async_remote_copy(
            src_ref=slabs.at[pl.ds(n * CAP, CAP)],
            dst_ref=got.at[pl.ds((REACH - o) * CAP, CAP)],
            send_sem=slab_s.at[n],
            recv_sem=slab_r.at[n],
            device_id=along(o),
            device_id_type=MESH,
        )
        copy.start()
        slab_copies.append(copy)
    for m in range(CAP):
        entry(REACH * CAP + m, got, REACH * CAP + m)
    load_recv.wait()
    load_flag.wait()
    peak[1] = take_peaks(0)
    send_peaks(1)
    for c in want_copies:
        c.wait_recv()
    second_block = [want_in[n] > 0.5 for n in range(2)]
    for n in range(2):
        pick = second_block[n]
        for f in range(5):
            for t in range(4):
                at = f * 64 + t * 16
                one, two = turns[at : at + 8], turns[at + 8 : at + 16]
                one = jnp.where(pick, pltpu.roll(one, 6, 0), one)
                two = jnp.where(pick, two, pltpu.roll(two, 2, 0))
                stage_x[n, f, t] = jnp.where((row & 2) == 0, one, two)
    def move(n, piece, source, target):
        copy = pltpu.make_async_remote_copy(
            src_ref=source,
            dst_ref=target,
            send_sem=move_s.at[n, piece],
            recv_sem=move_r.at[n, piece],
            device_id=along((-1, 1)[n]),
            device_id_type=MESH,
        )
        copy.start()
        return copy

    state_copies = [move(n, 3, stage_x.at[n], moved_ref.at[1 - n]) for n in range(2)]
    peak[2] = take_peaks(1)
    send_peaks(2)
    for c in slab_copies:
        c.wait_recv()
    rim_copies = []
    for a in range(3):
        for side in range(2):
            g = 2 * a + side
            for qa in range(2):
                pair = []
                for b in range(2):
                    at = (b * 6 + g) * 4 + 2 * qa
                    one, two = got[recv_ref[at]], got[recv_ref[at + 1]]
                    low = jnp.where(even, one, pltpu.roll(two, 8, 1))
                    high = jnp.where(even, pltpu.roll(one, 120, 1), two)
                    high = jnp.where(row == 7, scales[b], high)
                    ghosts[a][b, side, qa, 0:8] = low
                    ghosts[a][b, side, qa, 8:16] = high
                    pair.append((low, high))
                for n in range(2):
                    pick = second_block[n]
                    stage_g[a, n, side, qa, 0:8] = jnp.where(pick, pair[1][0], pair[0][0])
                    stage_g[a, n, side, qa, 8:16] = jnp.where(pick, pair[1][1], pair[0][1])
        rim_copies.append([move(n, a, stage_g.at[a, n], ghosts[a].at[3 - n]) for n in range(2)])
    slots = []
    for j in range(2):
        source = mig_ref[j]
        far = jnp.where(source // 2 < me, 2, 3)
        slots.append(jnp.where(source // 2 == me, source % 2, far))
    for c in state_copies:
        c.wait_recv()
    for f in range(5):
        planes = []
        for v in range(8):
            own = turns[f * 64 + v * 8 : f * 64 + v * 8 + 8]
            down, up = moved_ref[0, f, v // 2], moved_ref[1, f, v // 2]
            for b in range(2):
                away = 6 if b == 0 else 2
                mine = jnp.where(slots[b] == b, own, pltpu.roll(own, away, 0))
                other = jnp.where(slots[b] == 2, down, up)
                if v % 2 != b:
                    other = pltpu.roll(other, away, 0)
                value = jnp.where(slots[b] < 2, mine, other)
                both = value if b == 0 else jnp.where((row & 2) == 0, both, value)
            planes.append(both)
        for a in range(3):
            layout = planes if a == 0 else turned(planes, a, lane, row)
            up, down = (4, 4) if a == 0 else (1, 7)
            for v in range(8):
                cells[a, f, 3 + v] = layout[v]
            for layer in range(3):
                cells[a, f, 2 - layer] = pltpu.roll(layout[7 - layer], up, 0)
                cells[a, f, 11 + layer] = pltpu.roll(layout[layer], down, 0)
    def flux(a, p, u):
        inv = inverse(u[0])
        v = [u[1 + i] * inv for i in range(3)]
        kinetic = u[1] * v[0] + u[2] * v[1] + u[3] * v[2]
        pressure = 0.4 * (u[4] - 0.5 * kinetic)
        flow = [u[1 + a]] + [u[1 + i] * v[a] for i in range(3)] + [(u[4] + pressure) * v[a]]
        flow[1 + a] = flow[1 + a] + pressure
        for f in range(5):
            flows[a, f, p] = 0.5 * flow[f]

    for a in range(3):

        def inner(p, carry):
            flux(a, p, [cells[a, f, p] for f in range(5)])
            return carry

        lax.fori_loop(3, 11, inner, 0, unroll=4)
    top = take_peaks(2)
    half_fastest = 0.5 * jnp.max(jnp.where(upper, 0.0, top))
    step = 0.4 / jnp.full((8, 128), jnp.max(jnp.where(upper, top, 0.0)), F32)
    for a in range(3):
        for c in rim_copies[a]:
            c.wait_recv()
        for b in range(2):
            for side in range(2):
                for h in range(2):
                    base = a * 128 + row_of(a, side, b, h)
                    rims[pl.ds(base, 8, stride=8), :] = ghosts[a][slots[b], side, h, 0:8]
                    rims[pl.ds(base + 64, 8, stride=8), :] = ghosts[a][slots[b], side, h, 8:16]
        if a == 0:
            factor = step * rims[120:128]
        lower = (row & (4 if a == 0 else 1)) == 0
        for layer in range(3):
            rim = [rims[a * 128 + (f * 3 + layer) * 8 : a * 128 + (f * 3 + layer) * 8 + 8] for f in range(5)]
            low, high = 2 - layer, 11 + layer
            below = [jnp.where(lower, rim[f], cells[a, f, low]) for f in range(5)]
            above = [jnp.where(lower, cells[a, f, high], rim[f]) for f in range(5)]
            for f in range(5):
                cells[a, f, low] = below[f]
                cells[a, f, high] = above[f]
            flux(a, low, below)
            flux(a, high, above)

        def field(f, carry):
            flow, spread = flows[a, f], half_fastest * cells[a, f]
            hat = weno(flow + spread, 2, False) + weno(flow - spread, 3, True)
            change[a, f] = hat[1:] - hat[:-1]
            return carry

        lax.fori_loop(0, 5, field, 0)
    for f in range(5):
        second_part = turned_back([change[1, f, v] for v in range(8)], 1, lane, row)
        third_part = turned_back([change[2, f, v] for v in range(8)], 2, lane, row)
        for v in range(8):
            moved = change[0, f, v] + second_part[v] + third_part[v]
            result[f * 64 + v * 8 : f * 64 + v * 8 + 8] = cells[0, f, 3 + v] - factor * moved
    load_lane.wait()
    load_line.wait()
    halves = [plane_rows(result, 0, half) for half in range(2)]
    cubes = jnp.concatenate(
        [halves[half][n * 8 : n * 8 + 8] for n in range(10) for half in range(2)], 0
    )
    smooth = sum(dot(part, lane_ref[...]) for part in parts_of(2, cubes))
    smooth = sum(dot(line_ref[...], part) for part in parts_of(2, smooth))
    for b in range(2):
        kept = jnp.where(flag_ref[b] == 1, smooth[b * 80 : b * 80 + 80], cubes[b * 80 : b * 80 + 80])
        for f in range(5):
            for half in range(2):
                at = f * 16 + half * 8
                for h in range(2):
                    base = f * 64 + row_of(0, half, b, h)
                    result[pl.ds(base, 8, stride=8), :] = kept[at : at + 8, h * 128 : h * 128 + 128]
    for f in range(5):
        for c in range(32):
            at = f * 64 + (c // 2 % 8) * 8 + (c // 16) * 4 + c % 2
            out_ref[f, :, c * 128 : c * 128 + 128] = result[pl.ds(at, 2, stride=2), :]
    for phase in range(3):
        all_peaks(phase).wait_send()
    for c in want_copies + slab_copies + state_copies + [c for pair in rim_copies for c in pair]:
        c.wait_send()


def weno(values, centres, mirrored):
    half = 0.5 * (values[1:] - values[:-1])
    bend = half[1:] - half[:-1]
    rough = 1e-6 + (13.0 / 3.0) * (bend * bend)
    third = bend * (1.0 / 3.0)
    lo, n = centres, 9
    gl, gr = half[lo - 1 : lo - 1 + n], half[lo : lo + n]
    bl, bc, br = (slice(lo - 2 + t, lo - 2 + t + n) for t in range(3))
    tl = 2.0 * gl + bend[bl]
    tc = gl + gr
    tr = 2.0 * gr - bend[br]
    sl = rough[bl] + tl * tl
    sc = rough[bc] + tc * tc
    sr = rough[br] + tr * tr
    il = pl.reciprocal(sl, approx=True)
    ic = pl.reciprocal(sc, approx=True)
    ir = pl.reciprocal(sr, approx=True)
    wl, wc, wr = il * il, 6.0 * (ic * ic), ir * ir
    if mirrored:
        wl = 3.0 * wl
        cl = third[bl] + gl
        cc = third[bc] + gl
        cr = gr - 2.0 * third[br]
        total = wl * cl + wc * cc + wr * cr
        sign = -1.0
    else:
        wr = 3.0 * wr
        cl = gl + 2.0 * third[bl]
        cc = gr - third[bc]
        cr = gr - third[br]
        total = wl * cl + wc * cc + wr * cr
        sign = 1.0
    share = total * pl.reciprocal(wl + wc + wr, approx=True)
    centre = values[lo : lo + n]
    return centre + share if sign > 0 else centre - share


def solution(mesh):
    n_node, n_core = mesh.shape["node"], mesh.shape["cores"]
    nz = max(1, int(round(n_node**0.5)))
    tangents, picks = constant_tables()
    smoother = predict_table(8) @ np.eye(16)[0::2]
    lane_smoother = np.kron(smoother, smoother).T
    line_smoother = np.kron(np.eye(10), smoother)
    groups = n_core - 1 + nz - 1 + n_node // nz - 1

    def body(block_state, levels, send_table, receive_table, migration, coarsen_flags):
        state = pl.pallas_call(
            functools.partial(section_kernel, nz, n_node, n_core),
            out_shape=jax.ShapeDtypeStruct((5, 2, 4096), F32),
            in_specs=[HB] * 10,
            out_specs=VM,
            scratch_shapes=[
                pltpu.VMEM((5, 2, 4096), F32),
                pltpu.VMEM((960, 128), F32),
                pltpu.VMEM((3, 2, 192, 256), BF16),
                pltpu.VMEM((11, 12, 16, 128), F32),
                pltpu.VMEM((SLOTS - CAP, 8, 128), F32),
                pltpu.VMEM((SLOTS, 8, 128), F32),
                pltpu.VMEM((2, 8, 128), F32),
                pltpu.VMEM((2, 8, 128), F32),
                pltpu.VMEM((3, 2, 2, 2, 16, 128), F32),
                pltpu.VMEM((2, 5, 4, 8, 128), F32),
                [pltpu.VMEM((4, 2, 2, 16, 128), F32)] * 3,
                pltpu.VMEM((2, 5, 4, 8, 128), F32),
                pltpu.VMEM((3, 1, 128), F32),
                pltpu.VMEM((groups, 1, 128), F32),
                pltpu.VMEM((3, 5, 14, 8, 128), F32),
                pltpu.VMEM((3 * 16 * 8, 128), F32),
                pltpu.VMEM((3, 5, 14, 8, 128), F32),
                pltpu.VMEM((3, 5, 8, 8, 128), F32),
                pltpu.VMEM((320, 128), F32),
                pltpu.VMEM((256, 1536), BF16),
                pltpu.VMEM((2, 96, 80), BF16),
                pltpu.VMEM((256, 256), BF16),
                pltpu.VMEM((160, 160), BF16),
                pltpu.SMEM((5, SLOTS), jnp.int32),
                pltpu.SMEM((48,), jnp.int32),
                pltpu.SMEM((2,), jnp.int32),
                pltpu.SMEM((2,), jnp.int32),
                pltpu.SMEM((2,), jnp.int32),
                pltpu.SemaphoreType.DMA((6,)),
                pltpu.SemaphoreType.DMA((6,)),
                pltpu.SemaphoreType.DMA((2,)),
                pltpu.SemaphoreType.DMA((2,)),
                pltpu.SemaphoreType.DMA((2, 4)),
                pltpu.SemaphoreType.DMA((2, 4)),
                pltpu.SemaphoreType.DMA((3,)),
                pltpu.SemaphoreType.DMA((3,)),
                pltpu.SemaphoreType.DMA((10,)),
            ],
            compiler_params=pltpu.CompilerParams(
                collective_id=0, has_side_effects=True, vmem_limit_bytes=VMEM_BYTES
            ),
            name="section",
        )(
            jnp.transpose(block_state, (1, 0, 2)), send_table, receive_table, migration, levels, coarsen_flags,
            jnp.asarray(tangents, BF16), jnp.asarray(picks, BF16),
            jnp.asarray(lane_smoother, BF16), jnp.asarray(line_smoother, BF16),
        )
        return jnp.transpose(state, (1, 0, 2))

    both = ("node", "cores")
    return jax.shard_map(
        body,
        mesh=mesh,
        in_specs=(P(both, None, None), P(both), P(None, both), P(both), P(both), P(both)),
        out_specs=P(both, None, None),
        check_vma=False,
    )
```

```python
import functools

import jax
import jax.numpy as jnp
import numpy as np
from jax import lax
from jax.experimental import pallas as pl
from jax.experimental.pallas import tpu as pltpu
from jax.sharding import PartitionSpec as P

MESH = pl.DeviceIdType.MESH
F32 = jnp.float32
BF16 = jnp.bfloat16
EDGE = 16
REACH = 3
CAP = 7
VMEM_BYTES = 63 << 20
SLOTS = 49
VM = pl.BlockSpec(memory_space=pltpu.VMEM)
SM = pl.BlockSpec(memory_space=pltpu.SMEM)
HB = pl.BlockSpec(memory_space=pltpu.HBM)


def predict_table(n):
    w = np.zeros((2 * n, n))
    for c in range(n):
        w[2 * c, c] = 1.0
        if c == 0:
            w[1, 0:4] = np.array([5.0, 15.0, -5.0, 1.0]) / 16.0
        elif c == n - 2:
            w[2 * c + 1, n - 4 : n] = np.array([1.0, -5.0, 15.0, 5.0]) / 16.0
        elif c == n - 1:
            w[2 * c + 1, n - 1] = 1.0
        else:
            w[2 * c + 1, c - 1 : c + 3] = np.array([-1.0, 9.0, 9.0, -1.0]) / 16.0
    return w


def window_tables():
    depth = np.zeros((3, 3, 5))
    depth[0, :, 0:3] = np.eye(3)
    depth[1, :, 0:4] = predict_table(8)[0:3, 0:4]
    depth[2, 0, 0] = depth[2, 1, 2] = depth[2, 2, 4] = 1.0
    eye, fine = np.eye(16), predict_table(16)
    tangent = np.zeros((3, 4, 8, 16))
    for s in range(4):
        tangent[0, s] = eye[8 * (s % 2) : 8 * (s % 2) + 8]
        tangent[1, s] = fine[8 * s : 8 * s + 8]
        tangent[2, s] = eye[0::2]
    return depth, tangent


def constant_tables():
    depth, tangent = window_tables()
    pairs = [(0, s, 0) for s in range(2)]
    pairs += [(1, s, 2 * t) for s in range(4) for t in range(2)]
    pairs += [(2, 0, 0)]
    cols = []
    for kind, sa, sb in pairs:
        tile = np.zeros((16, 16, 8, 2, 8))
        for parity in range(2):
            tile[:, :, :, parity, :] = np.einsum(
                "pa,qb->abpq", tangent[kind, sa], tangent[kind, sb + parity]
            )
        cols.append(tile.reshape(256, 128))
    cols.append(np.zeros((256, 128)))
    tangents = np.concatenate(cols, 1)
    picks = np.zeros((2, 3, 2, 16, 10, 8))
    for kind in range(3):
        for b in range(2):
            for f in range(5):
                for i in range(3):
                    for layer in range(5):
                        picks[0, kind, b, f * 3 + i, b * 5 + f, layer] = depth[kind, i, layer]
                        picks[1, kind, b, f * 3 + i, b * 5 + f, 7 - layer] = depth[kind, i, layer]
    return tangents, picks.reshape(2, 96, 80)


def parts_of(count, x):
    parts = []
    for n in range(count):
        part = x.astype(BF16)
        parts.append(part)
        if n < count - 1:
            x = x - part.astype(F32)
    return parts


def dot(a, b):
    return jnp.dot(a, b, preferred_element_type=F32)


def iotas():
    lane = lax.broadcasted_iota(jnp.int32, (8, 128), 1)
    row = lax.broadcasted_iota(jnp.int32, (8, 128), 0)
    return lane, row


def inverse(x):
    guess = pl.reciprocal(x, approx=True)
    return guess * (2.0 - x * guess)


def swap(planes, lane, bit, reach):
    keep = (lane & reach) == 0
    out = list(planes)
    for v in range(8):
        if not (v >> bit) & 1:
            w = v | (1 << bit)
            out[v] = jnp.where(keep, planes[v], pltpu.roll(planes[w], reach, 1))
            out[w] = jnp.where(keep, pltpu.roll(planes[v], 128 - reach, 1), planes[w])
    return out


def swaps(planes, lane, reach):
    for bit in (2, 1, 0):
        planes = swap(planes, lane, bit, reach << bit)
    return planes


def cross(x, lane, row):
    odd = row & 1
    low = jnp.where(odd == 0, x, pltpu.roll(x, 1, 0))
    high = jnp.where(odd == 0, pltpu.roll(x, 7, 0), x)
    index = (lane & 7) * 16 + odd * 8 + lax.shift_right_logical(lane, 4)
    return jnp.where(
        (lane & 8) == 0,
        jnp.take_along_axis(low, index, axis=1),
        jnp.take_along_axis(high, index, axis=1),
    )


def turned(planes, dim, lane, row):
    if dim == 1:
        return swaps(planes, lane, 16)
    return [cross(x, lane, row) for x in swaps(planes, lane, 1)]


def turned_back(planes, dim, lane, row):
    if dim == 1:
        return swaps(planes, lane, 16)
    return swaps([cross(x, lane, row) for x in planes], lane, 1)


def row_of(dim, half, block, h):
    return half * 4 + block * 2 + h if dim == 0 else h * 4 + block * 2 + half


def plane_rows(ref, dim, half, base=0):
    return jnp.concatenate(
        [
            jnp.concatenate(
                [ref[pl.ds(base + f * 64 + row_of(dim, half, b, h), 8, stride=8), :] for h in range(2)], 1
            )
            for b in range(2)
            for f in range(5)
        ],
        0,
    )


def section_kernel(
    nz, n_node, n_core,
    x_hbm, send_hbm, recv_hbm, mig_hbm, level_hbm, flag_hbm, tan_hbm, pick_hbm, lane_hbm, line_hbm,
    out_ref,
    x_ref, turns, left, wide, slabs, got, want_out, want_in, stage_g, stage_x, ghosts, moved_ref, peak, peaks,
    cells, rims, flows, change, result, tan_ref, pick_ref, lane_ref, line_ref,
    send_ref, recv_ref, mig_ref, level_ref, flag_ref,
    slab_s, slab_r, want_s, want_r, move_s, move_r, peak_s, peak_r, load_s,
):
    node, core = lax.axis_index("node"), lax.axis_index("cores")
    me = node * n_core + core
    total = n_node * n_core
    ny = n_node // nz
    z, y = node % nz, node // nz
    lane, row = iotas()

    def along(offset):
        other = (me + offset + total) % total
        return (other // n_core, other % n_core)

    def around(count):
        return sorted(range(1, count), key=lambda t: (-min(t, count - t), t))

    groups = [
        [(node, (core + t) % n_core) for t in around(n_core)],
        [(y * nz + (z + t) % nz, core) for t in around(nz)],
        [(((y + t) % ny) * nz + z, core) for t in around(ny)],
    ]
    offsets = [side * o for o in range(REACH, 0, -1) for side in (-1, 1)]
    partners = [d for group in groups for d in group] + [along(o) for o in offsets]
    barrier = pltpu.get_barrier_semaphore()
    for d in partners:
        pl.semaphore_signal(barrier, inc=1, device_id=d, device_id_type=MESH)
    (load_x, load_level, load_mig, load_pick, load_send, load_tan, load_recv, load_flag, load_lane, load_line) = loads = [
        pltpu.make_async_copy(source, target, load_s.at[n])
        for n, (source, target) in enumerate(
            (
                (x_hbm, x_ref),
                (level_hbm, level_ref),
                (mig_hbm, mig_ref),
                (pick_hbm, pick_ref),
                (send_hbm, send_ref),
                (tan_hbm, tan_ref),
                (recv_hbm, recv_ref),
                (flag_hbm, flag_ref),
                (lane_hbm, lane_ref),
                (line_hbm, line_ref),
            )
        )
    ]
    for load in loads:
        load.start()

    firsts = [sum(len(g) for g in groups[:phase]) for phase in range(4)]

    def send_peaks(phase):
        for t, d in enumerate(groups[phase]):
            pltpu.make_async_remote_copy(
                src_ref=peak.at[phase],
                dst_ref=peaks.at[firsts[phase] + t],
                send_sem=peak_s.at[phase],
                recv_sem=peak_r.at[phase],
                device_id=d,
                device_id_type=MESH,
            ).start()

    def all_peaks(phase):
        slots = peaks.at[pl.ds(firsts[phase], len(groups[phase]))]
        return pltpu.make_async_remote_copy(
            src_ref=slots,
            dst_ref=slots,
            send_sem=peak_s.at[phase],
            recv_sem=peak_r.at[phase],
            device_id=groups[phase][0],
            device_id_type=MESH,
        )

    def take_peaks(phase):
        all_peaks(phase).wait_recv()
        best = peak[phase]
        for t in range(len(groups[phase])):
            best = jnp.maximum(best, peaks[firsts[phase] + t])
        return best

    load_x.wait()
    for f in range(5):
        for c in range(32):
            at = f * 64 + (c // 2 % 8) * 8 + (c // 16) * 4 + c % 2
            turns[pl.ds(at, 2, stride=2), :] = x_ref[f, :, c * 128 : c * 128 + 128]
    top = None
    for v in range(8):
        u = [turns[f * 64 + v * 8 : f * 64 + v * 8 + 8] for f in range(5)]
        inv = inverse(u[0])
        vel = [u[1 + i] * inv for i in range(3)]
        kinetic = u[1] * vel[0] + u[2] * vel[1] + u[3] * vel[2]
        pressure = 0.4 * (u[4] - 0.5 * kinetic)
        speed = jnp.maximum(jnp.maximum(jnp.abs(vel[0]), jnp.abs(vel[1])), jnp.abs(vel[2]))
        speed = speed + jnp.sqrt(1.4 * pressure * inv)
        top = speed if v == 0 else jnp.maximum(top, speed)
    load_level.wait()
    load_mig.wait()
    scales = [lax.shift_left(jnp.int32(EDGE), level_ref[b]).astype(F32) for b in range(2)]
    rated = top * jnp.where((row & 2) == 0, scales[0], scales[1])
    upper = (lane[0:1] & 64) != 0
    peak[0] = jnp.where(upper, jnp.max(rated), jnp.max(top))
    for n, direction in enumerate((1, -1)):
        want = jnp.int32(0)
        for j in range(2):
            source = mig_ref[j]
            want = want + jnp.where(source // 2 == me + direction, source % 2, 0)
        want_out[n] = jnp.full((8, 128), want, jnp.int32).astype(F32)
    pl.semaphore_wait(barrier, len(partners))
    send_peaks(0)
    want_copies = [
        pltpu.make_async_remote_copy(
            src_ref=want_out.at[n],
            dst_ref=want_in.at[n],
            send_sem=want_s.at[n],
            recv_sem=want_r.at[n],
            device_id=along(direction),
            device_id_type=MESH,
        )
        for n, direction in enumerate((1, -1))
    ]
    for c in want_copies:
        c.start()
    for f in range(5):
        planes = [turns[f * 64 + v * 8 : f * 64 + v * 8 + 8] for v in range(8)]
        for dim in (1, 2):
            for v, value in enumerate(turned(planes, dim, lane, row)):
                at = dim * 320 + f * 64 + v * 8
                turns[at : at + 8] = value
    load_pick.wait()
    for g in range(6):
        side = g % 2
        parts = parts_of(2, plane_rows(turns, g // 2, side, (g // 2) * 320))
        rows = sum(dot(pick_ref[side], part) for part in parts)
        for n, part in enumerate(parts_of(2, rows)):
            for kind in range(3):
                left[kind, n, g * 32 : g * 32 + 32] = part[kind * 32 : kind * 32 + 32]
    load_tan.wait()
    for tile in range(6):
        kind = 0 if tile == 0 else 1 if tile < 5 else 2
        weights = tan_ref[:, tile * 256 : tile * 256 + 256]
        out = sum(dot(left[kind, n], weights) for n in range(2))
        wide[2 * tile] = out[:, 0:128].reshape(12, 16, 128)
        if tile < 5:
            wide[2 * tile + 1] = out[:, 128:256].reshape(12, 16, 128)
    even = (lane & 8) == 0
    load_send.wait()

    def entry(k, into, at):
        blk, g, kind = send_ref[0, k], send_ref[1, k], send_ref[2, k]
        sa, sb = send_ref[3, k], send_ref[4, k]
        pair = jnp.where(kind == 0, sa % 2, jnp.where(kind == 1, 2 + sa * 2 + sb // 2, 10))
        parity = jnp.where(kind == 2, 0, sb % 2)
        low = wide[pair, g * 2 + blk, 0:8]
        high = wide[pair, g * 2 + blk, 8:16]
        ahead = jnp.where(even, low, pltpu.roll(high, 8, 1))
        behind = jnp.where(even, pltpu.roll(low, 120, 1), high)
        into[at] = jnp.where(jnp.full((8, 128), parity, jnp.int32) == 0, ahead, behind)

    slab_copies = []
    for n, o in enumerate(offsets):
        for m in range(CAP):
            entry((o + REACH) * CAP + m, slabs, n * CAP + m)
        copy = pltpu.make_async_remote_copy(
            src_ref=slabs.at[pl.ds(n * CAP, CAP)],
            dst_ref=got.at[pl.ds((REACH - o) * CAP, CAP)],
            send_sem=slab_s.at[n],
            recv_sem=slab_r.at[n],
            device_id=along(o),
            device_id_type=MESH,
        )
        copy.start()
        slab_copies.append(copy)
    for m in range(CAP):
        entry(REACH * CAP + m, got, REACH * CAP + m)
    load_recv.wait()
    load_flag.wait()
    peak[1] = take_peaks(0)
    send_peaks(1)
    for c in want_copies:
        c.wait_recv()
    second_block = [want_in[n] > 0.5 for n in range(2)]
    for n in range(2):
        pick = second_block[n]
        for f in range(5):
            for t in range(4):
                at = f * 64 + t * 16
                one, two = turns[at : at + 8], turns[at + 8 : at + 16]
                one = jnp.where(pick, pltpu.roll(one, 6, 0), one)
                two = jnp.where(pick, two, pltpu.roll(two, 2, 0))
                stage_x[n, f, t] = jnp.where((row & 2) == 0, one, two)
    def move(n, piece, source, target):
        copy = pltpu.make_async_remote_copy(
            src_ref=source,
            dst_ref=target,
            send_sem=move_s.at[n, piece],
            recv_sem=move_r.at[n, piece],
            device_id=along((-1, 1)[n]),
            device_id_type=MESH,
        )
        copy.start()
        return copy

    state_copies = [move(n, 3, stage_x.at[n], moved_ref.at[1 - n]) for n in range(2)]
    peak[2] = take_peaks(1)
    send_peaks(2)
    for c in slab_copies:
        c.wait_recv()
    rim_copies = []
    for a in range(3):
        for side in range(2):
            g = 2 * a + side
            for qa in range(2):
                pair = []
                for b in range(2):
                    at = (b * 6 + g) * 4 + 2 * qa
                    one, two = got[recv_ref[at]], got[recv_ref[at + 1]]
                    low = jnp.where(even, one, pltpu.roll(two, 8, 1))
                    high = jnp.where(even, pltpu.roll(one, 120, 1), two)
                    high = jnp.where(row == 7, scales[b], high)
                    ghosts[a][b, side, qa, 0:8] = low
                    ghosts[a][b, side, qa, 8:16] = high
                    pair.append((low, high))
                for n in range(2):
                    pick = second_block[n]
                    stage_g[a, n, side, qa, 0:8] = jnp.where(pick, pair[1][0], pair[0][0])
                    stage_g[a, n, side, qa, 8:16] = jnp.where(pick, pair[1][1], pair[0][1])
        rim_copies.append([move(n, a, stage_g.at[a, n], ghosts[a].at[3 - n]) for n in range(2)])
    slots = []
    for j in range(2):
        source = mig_ref[j]
        far = jnp.where(source // 2 < me, 2, 3)
        slots.append(jnp.where(source // 2 == me, source % 2, far))
    for c in state_copies:
        c.wait_recv()
    for f in range(5):
        planes = []
        for v in range(8):
            own = turns[f * 64 + v * 8 : f * 64 + v * 8 + 8]
            down, up = moved_ref[0, f, v // 2], moved_ref[1, f, v // 2]
            for b in range(2):
                away = 6 if b == 0 else 2
                mine = jnp.where(slots[b] == b, own, pltpu.roll(own, away, 0))
                other = jnp.where(slots[b] == 2, down, up)
                if v % 2 != b:
                    other = pltpu.roll(other, away, 0)
                value = jnp.where(slots[b] < 2, mine, other)
                both = value if b == 0 else jnp.where((row & 2) == 0, both, value)
            planes.append(both)
        for a in range(3):
            layout = planes if a == 0 else turned(planes, a, lane, row)
            up, down = (4, 4) if a == 0 else (1, 7)
            for v in range(8):
                cells[a, f, 3 + v] = layout[v]
            for layer in range(3):
                cells[a, f, 2 - layer] = pltpu.roll(layout[7 - layer], up, 0)
                cells[a, f, 11 + layer] = pltpu.roll(layout[layer], down, 0)
    def flux(a, p, u):
        inv = inverse(u[0])
        v = [u[1 + i] * inv for i in range(3)]
        kinetic = u[1] * v[0] + u[2] * v[1] + u[3] * v[2]
        pressure = 0.4 * (u[4] - 0.5 * kinetic)
        flow = [u[1 + a]] + [u[1 + i] * v[a] for i in range(3)] + [(u[4] + pressure) * v[a]]
        flow[1 + a] = flow[1 + a] + pressure
        for f in range(5):
            flows[a, f, p] = 0.5 * flow[f]

    for a in range(3):

        def inner(p, carry):
            flux(a, p, [cells[a, f, p] for f in range(5)])
            return carry

        lax.fori_loop(3, 11, inner, 0, unroll=8)
    top = jnp.broadcast_to(take_peaks(2), (8, 128))
    other_half = pltpu.roll(top, 64, 1)
    half_fastest = 0.5 * jnp.where((lane & 64) != 0, other_half, top)
    step = 0.4 / jnp.where((lane & 64) != 0, top, other_half)
    for a in range(3):
        for c in rim_copies[a]:
            c.wait_recv()
        for b in range(2):
            for side in range(2):
                for h in range(2):
                    base = a * 128 + row_of(a, side, b, h)
                    rims[pl.ds(base, 8, stride=8), :] = ghosts[a][slots[b], side, h, 0:8]
                    rims[pl.ds(base + 64, 8, stride=8), :] = ghosts[a][slots[b], side, h, 8:16]
        if a == 0:
            factor = step * rims[120:128]
        lower = (row & (4 if a == 0 else 1)) == 0
        for layer in range(3):
            rim = [rims[a * 128 + (f * 3 + layer) * 8 : a * 128 + (f * 3 + layer) * 8 + 8] for f in range(5)]
            low, high = 2 - layer, 11 + layer
            below = [jnp.where(lower, rim[f], cells[a, f, low]) for f in range(5)]
            above = [jnp.where(lower, cells[a, f, high], rim[f]) for f in range(5)]
            for f in range(5):
                cells[a, f, low] = below[f]
                cells[a, f, high] = above[f]
            flux(a, low, below)
            flux(a, high, above)

        def field(f, carry):
            flow, spread = flows[a, f], half_fastest * cells[a, f]
            hat = weno(flow + spread, 2, False) + weno(flow - spread, 3, True)
            change[a, f] = hat[1:] - hat[:-1]
            return carry

        lax.fori_loop(0, 5, field, 0, unroll=5)
    for f in range(5):
        second_part = turned_back([change[1, f, v] for v in range(8)], 1, lane, row)
        third_part = turned_back([change[2, f, v] for v in range(8)], 2, lane, row)
        for v in range(8):
            moved = change[0, f, v] + second_part[v] + third_part[v]
            result[f * 64 + v * 8 : f * 64 + v * 8 + 8] = cells[0, f, 3 + v] - factor * moved
    load_lane.wait()
    load_line.wait()
    halves = [plane_rows(result, 0, half) for half in range(2)]
    cubes = jnp.concatenate(
        [halves[half][n * 8 : n * 8 + 8] for n in range(10) for half in range(2)], 0
    )
    smooth = sum(dot(part, lane_ref[...]) for part in parts_of(2, cubes))
    smooth = sum(dot(line_ref[...], part) for part in parts_of(2, smooth))
    for b in range(2):
        kept = jnp.where(flag_ref[b] == 1, smooth[b * 80 : b * 80 + 80], cubes[b * 80 : b * 80 + 80])
        for f in range(5):
            for half in range(2):
                at = f * 16 + half * 8
                for h in range(2):
                    base = f * 64 + row_of(0, half, b, h)
                    result[pl.ds(base, 8, stride=8), :] = kept[at : at + 8, h * 128 : h * 128 + 128]
    for f in range(5):
        for c in range(32):
            at = f * 64 + (c // 2 % 8) * 8 + (c // 16) * 4 + c % 2
            out_ref[f, :, c * 128 : c * 128 + 128] = result[pl.ds(at, 2, stride=2), :]
    for phase in range(3):
        all_peaks(phase).wait_send()
    for c in want_copies + slab_copies + state_copies + [c for pair in rim_copies for c in pair]:
        c.wait_send()


def weno(values, centres, mirrored):
    half = 0.5 * (values[1:] - values[:-1])
    bend = half[1:] - half[:-1]
    rough = 1e-6 + (13.0 / 3.0) * (bend * bend)
    third = bend * (1.0 / 3.0)
    lo, n = centres, 9
    gl, gr = half[lo - 1 : lo - 1 + n], half[lo : lo + n]
    bl, bc, br = (slice(lo - 2 + t, lo - 2 + t + n) for t in range(3))
    tl = 2.0 * gl + bend[bl]
    tc = gl + gr
    tr = 2.0 * gr - bend[br]
    sl = rough[bl] + tl * tl
    sc = rough[bc] + tc * tc
    sr = rough[br] + tr * tr
    il = pl.reciprocal(sl, approx=True)
    ic = pl.reciprocal(sc, approx=True)
    ir = pl.reciprocal(sr, approx=True)
    wl, wc, wr = il * il, 6.0 * (ic * ic), ir * ir
    if mirrored:
        wl = 3.0 * wl
        cl = third[bl] + gl
        cc = third[bc] + gl
        cr = gr - 2.0 * third[br]
        total = wl * cl + wc * cc + wr * cr
        sign = -1.0
    else:
        wr = 3.0 * wr
        cl = gl + 2.0 * third[bl]
        cc = gr - third[bc]
        cr = gr - third[br]
        total = wl * cl + wc * cc + wr * cr
        sign = 1.0
    share = total * pl.reciprocal(wl + wc + wr, approx=True)
    centre = values[lo : lo + n]
    return centre + share if sign > 0 else centre - share


def solution(mesh):
    n_node, n_core = mesh.shape["node"], mesh.shape["cores"]
    nz = max(1, int(round(n_node**0.5)))
    tangents, picks = constant_tables()
    smoother = predict_table(8) @ np.eye(16)[0::2]
    lane_smoother = np.kron(smoother, smoother).T
    line_smoother = np.kron(np.eye(10), smoother)
    groups = n_core - 1 + nz - 1 + n_node // nz - 1

    def body(block_state, levels, send_table, receive_table, migration, coarsen_flags):
        state = pl.pallas_call(
            functools.partial(section_kernel, nz, n_node, n_core),
            out_shape=jax.ShapeDtypeStruct((5, 2, 4096), F32),
            in_specs=[HB] * 10,
            out_specs=VM,
            scratch_shapes=[
                pltpu.VMEM((5, 2, 4096), F32),
                pltpu.VMEM((960, 128), F32),
                pltpu.VMEM((3, 2, 192, 256), BF16),
                pltpu.VMEM((11, 12, 16, 128), F32),
                pltpu.VMEM((SLOTS - CAP, 8, 128), F32),
                pltpu.VMEM((SLOTS, 8, 128), F32),
                pltpu.VMEM((2, 8, 128), F32),
                pltpu.VMEM((2, 8, 128), F32),
                pltpu.VMEM((3, 2, 2, 2, 16, 128), F32),
                pltpu.VMEM((2, 5, 4, 8, 128), F32),
                [pltpu.VMEM((4, 2, 2, 16, 128), F32)] * 3,
                pltpu.VMEM((2, 5, 4, 8, 128), F32),
                pltpu.VMEM((3, 1, 128), F32),
                pltpu.VMEM((groups, 1, 128), F32),
                pltpu.VMEM((3, 5, 14, 8, 128), F32),
                pltpu.VMEM((3 * 16 * 8, 128), F32),
                pltpu.VMEM((3, 5, 14, 8, 128), F32),
                pltpu.VMEM((3, 5, 8, 8, 128), F32),
                pltpu.VMEM((320, 128), F32),
                pltpu.VMEM((256, 1536), BF16),
                pltpu.VMEM((2, 96, 80), BF16),
                pltpu.VMEM((256, 256), BF16),
                pltpu.VMEM((160, 160), BF16),
                pltpu.SMEM((5, SLOTS), jnp.int32),
                pltpu.SMEM((48,), jnp.int32),
                pltpu.SMEM((2,), jnp.int32),
                pltpu.SMEM((2,), jnp.int32),
                pltpu.SMEM((2,), jnp.int32),
                pltpu.SemaphoreType.DMA((6,)),
                pltpu.SemaphoreType.DMA((6,)),
                pltpu.SemaphoreType.DMA((2,)),
                pltpu.SemaphoreType.DMA((2,)),
                pltpu.SemaphoreType.DMA((2, 4)),
                pltpu.SemaphoreType.DMA((2, 4)),
                pltpu.SemaphoreType.DMA((3,)),
                pltpu.SemaphoreType.DMA((3,)),
                pltpu.SemaphoreType.DMA((10,)),
            ],
            compiler_params=pltpu.CompilerParams(
                collective_id=0, has_side_effects=True, vmem_limit_bytes=VMEM_BYTES
            ),
            name="section",
        )(
            jnp.transpose(block_state, (1, 0, 2)), send_table, receive_table, migration, levels, coarsen_flags,
            jnp.asarray(tangents, BF16), jnp.asarray(picks, BF16),
            jnp.asarray(lane_smoother, BF16), jnp.asarray(line_smoother, BF16),
        )
        return jnp.transpose(state, (1, 0, 2))

    both = ("node", "cores")
    return jax.shard_map(
        body,
        mesh=mesh,
        in_specs=(P(both, None, None), P(both), P(None, both), P(both), P(both), P(both)),
        out_specs=P(both, None, None),
        check_vma=False,
    )
```
